512 devices in a mesh: outer: 16 (over x, y), tp: 32 (over z, core).
Axes of the slice: x: 4, y: 4, z: 16, core: 2. Of those that a mesh axis runs over, the one named last changes fastest.
Arguments:
- activations: bfloat16 [4096, 4096], P('outer', 'tp'), may hold values from -6 to 6
- grads_out: bfloat16 [4096, 16384], P('outer', 'tp'), may hold values from -0.375 to 0.375
- feedback: bfloat16 [65536, 16384], P('outer', 'tp'), may hold values from -12 to 12
- start_right: float32 [16384, 64], P('tp'), may hold values from -0.046875 to 0.046875
Outputs:
- decompressed: bfloat16 [4096, 16384], P('outer', 'tp')
- right_factor: float32 [16384, 64], P('tp')
The draws below stay inside these ranges and needn't reach their ends.
All inputs are finite; a program needn't handle non-finite values.
Results may differ from the reference program's by a relative error of at most 0.001.
Values may be sent and summed in bfloat16 or wider, within the bound.
No kernel may reach another device: no remote copies, remote signals or barrier semaphores. Data moves between devices by JAX's collectives and lax.ppermute only.
A program may use at most 64 MiB of HBM per device.

```python
import jax
import jax.numpy as jnp
from jax import lax

D = 4096
FF = 16384
RANK = 64
TOK = 256
TOKENS = 4096
FEED_ROWS = 65536
N_OUTER = 16


def spiked(entries, rng, source, target, blocks, factor):
    def block_of(position):
        return (jnp.arange(entries.shape[position]) // (entries.shape[position] // blocks)).reshape((-1,) + (1,) * (entries.ndim - 1 - position))

    first = jax.random.permutation(rng, blocks)[block_of(target)]
    far = (block_of(target) + blocks // 2) % blocks
    return jnp.where((block_of(source) == first) | (block_of(source) == far), factor * entries, entries)


def shard_levels(stream_key, extent, split, smallest, top_value):
    def one(dim, blocks):
        steps = jax.random.uniform(jax.random.fold_in(jax.random.fold_in(stream_key, 6), dim), (blocks,), jnp.float32, smallest / len(split), top_value / len(split))
        return jnp.repeat(jnp.exp(steps), extent[dim] // blocks).reshape((-1,) + (1,) * (len(extent) - dim - 1))

    loudness = one(*split[0])
    for cut in split[1:]:
        loudness = loudness * one(*cut)
    return loudness


def noise(own_key, dims, deviation, most, cuts=(), held_as=jnp.bfloat16):
    result = jax.random.normal(own_key, dims, jnp.float32) * deviation
    if len(cuts) > 0:
        result = shard_levels(own_key, dims, cuts, -0.22, 0.18) * result
    return jnp.clip(result, min=-most, max=most).astype(held_as)


def bell_draw_with(key, dims, deviation, reach, cuts, heavy, dtype=jnp.bfloat16):
    entries = deviation * jax.random.normal(key, dims, jnp.float32)
    if cuts:
        entries = entries * shard_levels(key, dims, cuts, -0.22, 0.18)
    return jnp.clip(spiked(entries, jax.random.fold_in(key, 3), *heavy), -reach, reach).astype(dtype)


def setup_inputs(seed: int = 0) -> dict:
    keys = jax.random.split(jax.random.key(seed), 5)
    return {
        "activations": bell_draw_with(keys[0], (TOKENS, D), 1.0, 6.0, ((0, 16), (1, 32)), (0, 1, 32, 2.75)),
        "grads_out": noise(keys[1], (TOKENS, FF), (TOK ** -0.5), 0.375, ((0, 16), (1, 32))),
        "feedback": noise(keys[2], (FEED_ROWS, FF), 2.0, 12.0, ((0, 16), (1, 32))),
        "start_right": noise(keys[3], (FF, RANK), FF ** -0.5, 0.046875, ((0, 32),), jnp.float32),
    }


def reference(activations, grads_out, feedback, start_right):
    summed = jnp.dot(activations.T.astype(jnp.float32), grads_out.astype(jnp.float32), preferred_element_type=jnp.float32)
    summed = summed + jnp.sum(feedback.astype(jnp.float32).reshape(N_OUTER, D, FF), axis=0)
    left = jnp.dot(summed, start_right, precision=lax.Precision.HIGHEST)
    gram_matrix = jnp.dot(left.T, left, precision=lax.Precision.HIGHEST)
    factor = jnp.linalg.cholesky(gram_matrix)
    basis = jax.scipy.linalg.solve_triangular(factor, left.T, lower=True).T
    right_factor = jnp.dot(summed.T, basis, precision=lax.Precision.HIGHEST)
    decompressed = jnp.dot(basis, right_factor.T, precision=lax.Precision.HIGHEST).astype(jnp.bfloat16)
    return (decompressed, right_factor)
```

```python
import jax
import jax.numpy as jnp
from jax import lax
from jax.experimental import pallas as pl
from jax.experimental.pallas import tpu as pltpu
from jax.sharding import Mesh
from jax.sharding import PartitionSpec as P

F32 = jnp.float32
BF16 = jnp.bfloat16
LANES = 128
XYC = ("x", "y", "c")
XY = ("x", "y")
FAST = dict(preferred_element_type=F32)
FULL = dict(preferred_element_type=F32, precision=lax.Precision.HIGHEST)


def nn(a, b, kind=FAST):
    return lax.dot_general(a, b, (((1,), (0,)), ((), ())), **kind)


def nt(a, b, kind=FAST):
    return lax.dot_general(a, b, (((1,), (1,)), ((), ())), **kind)


def tn(a, b, kind=FAST):
    return lax.dot_general(a, b, (((0,), (0,)), ((), ())), **kind)


def pieces(value):
    high = value.astype(BF16)
    rest = value - high.astype(F32)
    middle = rest.astype(BF16)
    low = (rest - middle.astype(F32)).astype(BF16)
    return jnp.concatenate([high, middle, low], axis=0)


def folded(stacked):
    third = stacked.shape[0] // 3
    return stacked[:third] + (stacked[third : 2 * third] + stacked[2 * third :])


def cost(flops, count):
    return pl.CostEstimate(flops=flops, bytes_accessed=count, transcendentals=0)


def project(start_right, grads):
    width, rank = start_right.shape
    tokens = grads.shape[0]

    def kernel(start_ref, grads_ref, split_ref, out_ref):
        split = pieces(start_ref[...].T)
        split_ref[...] = split
        result = folded(nt(split, grads_ref[...]))
        half = tokens // 2
        out_ref[0] = result[:, :half]
        out_ref[1] = result[:, half:]

    return pl.pallas_call(
        kernel,
        out_shape=(
            jax.ShapeDtypeStruct((3 * rank, width), BF16),
            jax.ShapeDtypeStruct((2, rank, tokens // 2), F32),
        ),
        cost_estimate=cost(6 * rank * width * tokens, 2 * grads.size + 8 * start_right.size),
        name="project",
    )(start_right, grads)


def feedback_left(split, feedback, group):
    rows, width = feedback.shape
    rank = split.shape[0] // 3

    def kernel(split_ref, feed_ref, out_ref):
        result = folded(nt(split_ref[...], feed_ref[...]))
        for i in range(group):
            out_ref[i] = result[:, i * LANES : (i + 1) * LANES]

    return pl.pallas_call(
        kernel,
        grid=(rows // (group * LANES),),
        in_specs=[
            pl.BlockSpec(split.shape, lambda i: (0, 0)),
            pl.BlockSpec((group * LANES, width), lambda i: (i, 0)),
        ],
        out_specs=pl.BlockSpec((group, rank, LANES), lambda i: (i, 0, 0)),
        out_shape=jax.ShapeDtypeStruct((rows // LANES, rank, LANES), F32),
        cost_estimate=cost(6 * rank * width * rows, 2 * feedback.size + 4 * rows * rank),
        name="feedback_left",
    )(split, feedback)


def add_activations(place, shares, columns, partial):
    ways, rank, tokens = shares.shape

    def kernel(place_ref, shares_ref, columns_ref, partial_ref, out_ref):
        total = shares_ref[0]
        for i in range(1, ways):
            total = total + shares_ref[i]
        out_ref[0] = partial_ref[0] + folded(nn(pieces(total), columns_ref[0]))

    block = pl.BlockSpec((1, rank, LANES), lambda i, place: (2 * place[0] + i, 0, 0))
    return pl.pallas_call(
        kernel,
        grid_spec=pltpu.PrefetchScalarGridSpec(
            num_scalar_prefetch=1,
            grid=(2,),
            in_specs=[
                pl.BlockSpec(shares.shape, lambda i, place: (0, 0, 0)),
                pl.BlockSpec((1, tokens, LANES), lambda i, place: (i, 0, 0)),
                block,
            ],
            out_specs=block,
        ),
        out_shape=jax.ShapeDtypeStruct(partial.shape, F32),
        input_output_aliases={3: 0},
        cost_estimate=cost(12 * rank * tokens * LANES, 4 * shares.size),
        name="add_activations",
    )(place, shares, columns, partial)


def summed_copies(shares, copies):
    ways, rows, lanes = shares.shape

    def kernel(shares_ref, out_ref):
        total = shares_ref[0]
        for i in range(1, ways):
            total = total + shares_ref[i]
        for i in range(copies):
            out_ref[i] = total

    return pl.pallas_call(
        kernel,
        out_shape=jax.ShapeDtypeStruct((copies, rows, lanes), F32),
        cost_estimate=cost(shares.size, 4 * shares.size),
        name="summed_copies",
    )(shares)


def right_products(left, feedback, activations, grads, group, parts):
    blocks, rank, _ = left.shape
    rows, width = feedback.shape
    tokens = grads.shape[0]
    steps = blocks // group
    split_rows = rank * width // (256 * parts)
    across = width // 256

    def kernel(left_ref, feed_ref, act_ref, grads_ref, out_ref, gram_ref, right, inner, gram):
        step = pl.program_id(0)

        @pl.when(step == 0)
        def _():
            right[...] = jnp.zeros_like(right)
            inner[...] = jnp.zeros_like(inner)
            gram[...] = jnp.zeros_like(gram)

        split = pieces(jnp.concatenate([left_ref[i] for i in range(group)], axis=1))
        cols = jnp.concatenate([act_ref[i] for i in range(group)], axis=1)
        right[...] += nn(split, feed_ref[...])
        inner[...] += nt(split, cols)
        gram[...] += nt(split, split)

        @pl.when(step == steps - 1)
        def _():
            total = folded(right[...] + nn(pieces(folded(inner[...])), grads_ref[...]))
            for i in range(parts):
                down, over = i // across, i % across
                out_ref[i] = total[
                    down * split_rows : (down + 1) * split_rows, over * 256 : (over + 1) * 256
                ]
            square = folded(gram[...])
            gram_ref[...] = (
                square[:, :rank] + square[:, rank : 2 * rank] + square[:, 2 * rank :]
            )

    return pl.pallas_call(
        kernel,
        grid=(steps,),
        in_specs=[
            pl.BlockSpec((group, rank, LANES), lambda i: (i, 0, 0)),
            pl.BlockSpec((group * LANES, width), lambda i: (i, 0)),
            pl.BlockSpec((group, tokens, LANES), lambda i: (i, 0, 0)),
            pl.BlockSpec(grads.shape, lambda i: (0, 0)),
        ],
        out_specs=[
            pl.BlockSpec((parts, split_rows, 256), lambda i: (0, 0, 0)),
            pl.BlockSpec((rank, rank), lambda i: (0, 0)),
        ],
        out_shape=(
            jax.ShapeDtypeStruct((parts, split_rows, 256), F32),
            jax.ShapeDtypeStruct((rank, rank), F32),
        ),
        scratch_shapes=[
            pltpu.VMEM((3 * rank, width), F32),
            pltpu.VMEM((3 * rank, tokens), F32),
            pltpu.VMEM((3 * rank, 3 * rank), F32),
        ],
        cost_estimate=cost(
            6 * rank * rows * (width + tokens + 3 * rank), 2 * feedback.size + 2 * activations.size
        ),
        name="right_products",
    )(left, feedback, activations, grads)


def inverse_factor(gram):
    rank = gram.shape[0]

    def kernel(gram_ref, out_ref):
        row = lax.broadcasted_iota(jnp.int32, (rank, rank), 0)
        col = lax.broadcasted_iota(jnp.int32, (rank, rank), 1)
        work = jnp.concatenate([gram_ref[...], (row == col).astype(F32)], axis=1)
        index = lax.broadcasted_iota(jnp.int32, (rank, 1), 0)
        for k in range(rank):
            low = k // 8 * 8
            pivot_row = work[k : k + 1]
            scale = 1.0 / work[k : k + 1, k : k + 1]
            part = work[low:]
            factor = jnp.where(index[low:] > k, part[:, k : k + 1] * scale, 0.0)
            part = part - factor * pivot_row
            work = part if low == 0 else jnp.concatenate([work[:low], part], axis=0)
        diagonal = jnp.sum(jnp.where(row == col, work[:, :rank], 0.0), axis=1, keepdims=True)
        out_ref[...] = work[:, rank:] / jnp.sqrt(diagonal)

    return pl.pallas_call(
        kernel,
        out_shape=jax.ShapeDtypeStruct((rank, rank), F32),
        cost_estimate=cost(2 * rank * rank * rank * 8, 8 * rank * rank),
        name="inverse_factor",
    )(gram)


def finish(place, inverse, left, gathered, width, slab):
    rank = inverse.shape[0]
    parts = gathered.shape[0]
    across = width // 256
    blocks = slab // LANES

    def kernel(place_ref, inverse_ref, left_ref, gathered_ref, dec_ref, right_ref):
        across_rows = [
            jnp.concatenate([gathered_ref[i + j] for j in range(across)], axis=1)
            for i in range(0, parts, across)
        ]
        right = nn(inverse_ref[...], jnp.concatenate(across_rows, axis=0), FULL)
        right_ref[...] = right.T
        rows = jnp.concatenate([left_ref[i] for i in range(blocks)], axis=1)
        basis = nn(inverse_ref[...], rows, FULL)
        dec_ref[...] = tn(basis, right, FULL).astype(BF16)

    return pl.pallas_call(
        kernel,
        grid_spec=pltpu.PrefetchScalarGridSpec(
            num_scalar_prefetch=1,
            grid=(1,),
            in_specs=[
                pl.BlockSpec(inverse.shape, lambda i, place: (0, 0)),
                pl.BlockSpec((blocks, rank, LANES), lambda i, place: (place[0], 0, 0)),
                pl.BlockSpec(gathered.shape, lambda i, place: (0, 0, 0)),
            ],
            out_specs=[
                pl.BlockSpec((slab, width), lambda i, place: (0, 0)),
                pl.BlockSpec((width, rank), lambda i, place: (0, 0)),
            ],
        ),
        out_shape=(
            jax.ShapeDtypeStruct((slab, width), BF16),
            jax.ShapeDtypeStruct((width, rank), F32),
        ),
        cost_estimate=cost(12 * rank * slab * width, 4 * gathered.size),
        name="finish",
    )(place, inverse, left, gathered)


def exchange(value, axes):
    return lax.all_to_all(value, axes, 0, 0, tiled=True)


def index_of(axes):
    return lax.axis_index(axes).astype(jnp.int32).reshape(1)


def per_device(activations, grads_out, feedback, start_right):
    tokens, lanes = activations.shape
    width = grads_out.shape[1]
    z_far, z_near = lax.axis_size("zh"), lax.axis_size("zl")
    groups = lax.axis_size(XYC)
    outer = lax.axis_size(XY)
    gathered = lax.all_gather(activations, ("zh", "zl", "c"), axis=0)
    columns = exchange(activations.reshape(2, tokens // 2, lanes), "c")

    split, inner = project(start_right, grads_out)
    inner = summed_copies(exchange(inner, "c"), z_near)
    inner = summed_copies(exchange(inner, "zl"), z_far)
    inner = exchange(inner, "zh")

    partial = feedback_left(split, feedback, 4)
    partial = add_activations(index_of(("zh", "zl")), inner, columns, partial)

    left = summed_copies(exchange(partial, XYC), z_near)
    left = summed_copies(exchange(left, "zl"), z_far)
    left = summed_copies(exchange(left, "zh"), groups)
    left = exchange(left, XYC)

    right, gram = right_products(left, feedback, gathered, grads_out, 4, outer)
    inverse = inverse_factor(gram)
    right = summed_copies(exchange(right, XY), outer)
    right = exchange(right, XY)
    return finish(index_of(XY), inverse, left, right, width, feedback.shape[0] // outer)


def solution(mesh):
    outer, tp = mesh.shape["outer"], mesh.shape["tp"]
    across = 4 if outer == 16 else 2
    near = 4 if tp == 32 else 2
    names = ("x", "y", "zh", "zl", "c")
    shape = (outer // across, across, tp // (2 * near), near, 2)
    split_mesh = Mesh(mesh.devices.reshape(shape), names)
    z = ("zh", "zl", "c")
    return jax.shard_map(
        per_device,
        mesh=split_mesh,
        in_specs=(P(XY, z), P(XY, z), P(XY, z), P(z, None)),
        out_specs=(P(XY, z), P(z, None)),
        check_vma=False,
    )
```

```python
import jax
import jax.numpy as jnp
from jax import lax
from jax.experimental import pallas as pl
from jax.experimental.pallas import tpu as pltpu
from jax.sharding import Mesh
from jax.sharding import PartitionSpec as P

F32 = jnp.float32
BF16 = jnp.bfloat16
LANES = 128
XY = ("x", "y")
FAST = dict(preferred_element_type=F32)
FULL = dict(preferred_element_type=F32, precision=lax.Precision.HIGHEST)


def nn(a, b, kind=FAST):
    return lax.dot_general(a, b, (((1,), (0,)), ((), ())), **kind)


def nt(a, b, kind=FAST):
    return lax.dot_general(a, b, (((1,), (1,)), ((), ())), **kind)


def tn(a, b, kind=FAST):
    return lax.dot_general(a, b, (((0,), (0,)), ((), ())), **kind)


def pieces(value):
    high = value.astype(BF16)
    rest = value - high.astype(F32)
    middle = rest.astype(BF16)
    low = (rest - middle.astype(F32)).astype(BF16)
    return jnp.concatenate([high, middle, low], axis=0)


def folded(stacked):
    third = stacked.shape[0] // 3
    return stacked[:third] + (stacked[third : 2 * third] + stacked[2 * third :])


PARAMS = pltpu.CompilerParams(vmem_limit_bytes=16 * 1024 * 1024)


def cost(flops, count):
    return pl.CostEstimate(flops=flops, bytes_accessed=count, transcendentals=0)


def project(start_right, grads, copies):
    rank, width = start_right.shape
    tokens = grads.shape[0]

    def kernel(start_ref, grads_ref, split_ref, out_ref):
        split = pieces(start_ref[...])
        split_ref[...] = split
        result = folded(nt(split, grads_ref[...]))
        for i in range(copies):
            out_ref[i] = result

    return pl.pallas_call(
        kernel,
        out_shape=(
            jax.ShapeDtypeStruct((3 * rank, width), BF16),
            jax.ShapeDtypeStruct((copies, rank, tokens), F32),
        ),
        cost_estimate=cost(6 * rank * width * tokens, 2 * grads.size + 8 * start_right.size),
        compiler_params=PARAMS,
        name="project",
    )(start_right, grads)


def feedback_left(half, split, feedback, pairs):
    rows, width = feedback.shape
    rank = split.shape[0] // 3

    def kernel(half_ref, split_ref, feed_ref, own_ref, other_ref):
        result = folded(nt(split_ref[...], feed_ref[...]))
        odd = half_ref[0] == 1
        for i in range(pairs):
            even_rows = result[:, 2 * i * LANES : (2 * i + 1) * LANES]
            odd_rows = result[:, (2 * i + 1) * LANES : (2 * i + 2) * LANES]
            own_ref[i] = jnp.where(odd, odd_rows, even_rows)
            other_ref[i] = jnp.where(odd, even_rows, odd_rows)

    block = pl.BlockSpec((pairs, rank, LANES), lambda i, half: (i, 0, 0))
    shape = jax.ShapeDtypeStruct((rows // (2 * LANES), rank, LANES), F32)
    return pl.pallas_call(
        kernel,
        grid_spec=pltpu.PrefetchScalarGridSpec(
            num_scalar_prefetch=1,
            grid=(rows // (2 * pairs * LANES),),
            in_specs=[
                pl.BlockSpec(split.shape, lambda i, half: (0, 0)),
                pl.BlockSpec((2 * pairs * LANES, width), lambda i, half: (i, 0)),
            ],
            out_specs=[block, block],
        ),
        out_shape=(shape, shape),
        cost_estimate=cost(6 * rank * width * rows, 2 * feedback.size + 4 * rows * rank),
        compiler_params=PARAMS,
        name="feedback_left",
    )(half, split, feedback)


def block_at(place_ref, step, far_size, near_size):
    far = lax.rem(place_ref[0] + step, far_size)
    return far * near_size + place_ref[1]


def whole_specs(count):
    scalar = pl.BlockSpec(memory_space=pltpu.SMEM)
    return [scalar] + [pl.BlockSpec(memory_space=pltpu.VMEM)] * count


def add_activations(place, shares, columns, own, other):
    ways, rank, tokens = shares.shape
    far_size, blocks = len(columns), own.shape[0]

    def kernel(place_ref, shares_ref, own_ref, other_ref, *refs):
        column_refs, out_ref = refs[:-1], refs[-1]
        for i in range(blocks):
            out_ref[i] = own_ref[i] + other_ref[i]
        total = shares_ref[0]
        for i in range(1, ways):
            total = total + shares_ref[i]
        across = jnp.concatenate([ref[...] for ref in column_refs], axis=1)
        extra = folded(nn(pieces(total), across))
        for i in range(far_size):
            block = block_at(place_ref, i, far_size, blocks // far_size)
            out_ref[block] = out_ref[block] + extra[:, i * LANES : (i + 1) * LANES]

    return pl.pallas_call(
        kernel,
        in_specs=whole_specs(3 + far_size),
        out_shape=jax.ShapeDtypeStruct(own.shape, F32),
        cost_estimate=cost(24 * rank * tokens * LANES, 12 * own.size),
        compiler_params=PARAMS,
        name="add_activations",
    )(place, shares, own, other, *columns)


def summed_copies(shares, copies):
    ways, rows, lanes = shares.shape

    def kernel(shares_ref, out_ref):
        total = shares_ref[0]
        for i in range(1, ways):
            total = total + shares_ref[i]
        for i in range(copies):
            out_ref[i] = total

    return pl.pallas_call(
        kernel,
        out_shape=jax.ShapeDtypeStruct((copies, rows, lanes), F32),
        cost_estimate=cost(shares.size, 4 * shares.size),
        compiler_params=PARAMS,
        name="summed_copies",
    )(shares)


def inner_products(place, left, columns, copies):
    blocks, rank, _ = left.shape
    far_size, tokens = len(columns), columns[0].shape[0]

    def kernel(place_ref, left_ref, *refs):
        column_refs, out_ref = refs[:-1], refs[-1]
        rows = [left_ref[block_at(place_ref, i, far_size, blocks // far_size)] for i in range(far_size)]
        across = jnp.concatenate([ref[...] for ref in column_refs], axis=1)
        result = folded(nt(pieces(jnp.concatenate(rows, axis=1)), across))
        for i in range(copies):
            out_ref[i] = result

    return pl.pallas_call(
        kernel,
        in_specs=whole_specs(1 + far_size),
        out_shape=jax.ShapeDtypeStruct((copies, rank, tokens), F32),
        cost_estimate=cost(6 * rank * tokens * far_size * LANES, 8 * columns[0].size),
        compiler_params=PARAMS,
        name="inner_products",
    )(place, left, *columns)


def feedback_right(half, left, feedback, group, before):
    blocks, rank, _ = left.shape
    rows, width = feedback.shape
    steps = blocks // group
    first = before is None

    def kernel(half_ref, left_ref, *refs):
        feeds, refs = refs[:group], refs[group:]
        old, (out_ref, gram_ref, right, gram) = refs[:-4], refs[-4:]
        step = pl.program_id(0)

        @pl.when(step == 0)
        def _():
            right[...] = jnp.zeros_like(right)
            gram[...] = jnp.zeros_like(gram)

        split = pieces(jnp.concatenate([left_ref[i] for i in range(group)], axis=1))
        right[...] += folded(nn(split, jnp.concatenate([feed[...] for feed in feeds], axis=0)))
        gram[...] += nt(split, split)

        @pl.when(step == steps - 1)
        def _():
            square = folded(gram[...])
            square = square[:, :rank] + square[:, rank : 2 * rank] + square[:, 2 * rank :]
            total = right[...]
            out_ref[...] = total if first else total + old[0][...]
            gram_ref[...] = square if first else square + old[1][...]

    whole = [
        pl.BlockSpec((rank, width), lambda i, half: (0, 0)),
        pl.BlockSpec((rank, rank), lambda i, half: (0, 0)),
    ]
    return pl.pallas_call(
        kernel,
        grid_spec=pltpu.PrefetchScalarGridSpec(
            num_scalar_prefetch=1,
            grid=(steps,),
            in_specs=[
                pl.BlockSpec((group, rank, LANES), lambda i, half: (i, 0, 0)),
            ]
            + [
                pl.BlockSpec((LANES, width), lambda i, half, j=j: (2 * (group * i + j) + half[0], 0))
                for j in range(group)
            ]
            + ([] if first else whole),
            out_specs=whole,
            scratch_shapes=[
                pltpu.VMEM((rank, width), F32),
                pltpu.VMEM((3 * rank, 3 * rank), F32),
            ],
        ),
        out_shape=(
            jax.ShapeDtypeStruct((rank, width), F32),
            jax.ShapeDtypeStruct((rank, rank), F32),
        ),
        cost_estimate=cost(3 * rank * rows * (width + 3 * rank), feedback.size),
        compiler_params=PARAMS,
        name="feedback_right",
    )(half, left, *([feedback] * group), *(before or ()))


def add_grads(shares, grads, partial, parts):
    ways, rank, tokens = shares.shape
    width = grads.shape[1]
    split_rows = rank * width // (256 * parts)
    across = width // 256

    def kernel(shares_ref, grads_ref, partial_ref, out_ref):
        inner = shares_ref[0]
        for i in range(1, ways):
            inner = inner + shares_ref[i]
        total = partial_ref[...] + folded(nn(pieces(inner), grads_ref[...]))
        for i in range(parts):
            down, over = i // across * split_rows, i % across * 256
            out_ref[i] = total[down : down + split_rows, over : over + 256]

    return pl.pallas_call(
        kernel,
        out_shape=jax.ShapeDtypeStruct((parts, split_rows, 256), F32),
        cost_estimate=cost(6 * rank * tokens * width, 4 * shares.size + 2 * grads.size),
        compiler_params=PARAMS,
        name="add_grads",
    )(shares, grads, partial)


def inverse_factor(gram):
    rank = gram.shape[0]

    def kernel(gram_ref, out_ref):
        row = lax.broadcasted_iota(jnp.int32, (rank, rank), 0)
        col = lax.broadcasted_iota(jnp.int32, (rank, rank), 1)
        work = jnp.concatenate([gram_ref[...], (row == col).astype(F32)], axis=1)
        index = lax.broadcasted_iota(jnp.int32, (rank, 1), 0)
        for k in range(rank):
            low = k // 8 * 8
            pivot_row = work[k : k + 1]
            scale = 1.0 / work[k : k + 1, k : k + 1]
            part = work[low:]
            factor = jnp.where(index[low:] > k, part[:, k : k + 1] * scale, 0.0)
            part = part - factor * pivot_row
            work = part if low == 0 else jnp.concatenate([work[:low], part], axis=0)
        diagonal = jnp.sum(jnp.where(row == col, work[:, :rank], 0.0), axis=1, keepdims=True)
        out_ref[...] = work[:, rank:] / jnp.sqrt(diagonal)

    return pl.pallas_call(
        kernel,
        out_shape=jax.ShapeDtypeStruct((rank, rank), F32),
        cost_estimate=cost(2 * rank * rank * rank * 8, 8 * rank * rank),
        compiler_params=PARAMS,
        name="inverse_factor",
    )(gram)


def finish(place, half, inverse, own, other, gathered, width):
    rank = inverse.shape[0]
    parts = gathered.shape[0]
    across = width // 256
    slab = 2 * LANES

    def kernel(place_ref, half_ref, inverse_ref, own_ref, other_ref, gathered_ref, dec_ref, right_ref):
        across_rows = [
            jnp.concatenate([gathered_ref[i + j] for j in range(across)], axis=1)
            for i in range(0, parts, across)
        ]
        right = nn(inverse_ref[...], jnp.concatenate(across_rows, axis=0), FULL)
        right_ref[...] = right
        odd = half_ref[0] == 1
        even_rows = jnp.where(odd, other_ref[0], own_ref[0])
        odd_rows = jnp.where(odd, own_ref[0], other_ref[0])
        basis = nn(inverse_ref[...], jnp.concatenate([even_rows, odd_rows], axis=1), FULL)
        dec_ref[...] = tn(basis, right, FULL).astype(BF16)

    block = pl.BlockSpec((1, rank, LANES), lambda i, place, half: (place[0], 0, 0))
    return pl.pallas_call(
        kernel,
        grid_spec=pltpu.PrefetchScalarGridSpec(
            num_scalar_prefetch=2,
            grid=(1,),
            in_specs=[
                pl.BlockSpec(inverse.shape, lambda i, place, half: (0, 0)),
                block,
                block,
                pl.BlockSpec(gathered.shape, lambda i, place, half: (0, 0, 0)),
            ],
            out_specs=[
                pl.BlockSpec((slab, width), lambda i, place, half: (0, 0)),
                pl.BlockSpec((rank, width), lambda i, place, half: (0, 0)),
            ],
        ),
        out_shape=(
            jax.ShapeDtypeStruct((slab, width), BF16),
            jax.ShapeDtypeStruct((rank, width), F32),
        ),
        cost_estimate=cost(12 * rank * slab * width, 4 * gathered.size),
        compiler_params=PARAMS,
        name="finish",
    )(place, half, inverse, own, other, gathered)


def exchange(value, axes):
    return lax.all_to_all(value, axes, 0, 0, tiled=True)


def index_of(axes):
    return lax.axis_index(axes).astype(jnp.int32).reshape(1)


def per_device(activations, grads_out, feedback, start_right):
    width = grads_out.shape[1]
    far, near = lax.axis_size("zh"), lax.axis_size("zl")
    outer = lax.axis_size(XY)
    place, half = jnp.concatenate([index_of("zh"), index_of("zl")]), index_of("c")

    columns = [activations] + [
        lax.ppermute(activations, "zh", [((i + j) % far, i) for i in range(far)])
        for j in range(1, far)
    ]
    split, inner = project(start_right.T, grads_out, 2 * near)
    inner = exchange(inner, ("zl", "c"))
    own, other = feedback_left(half, split, feedback, 2)
    other = lax.ppermute(other, "c", [(0, 1), (1, 0)])
    left = add_activations(place, inner, columns, own, other)

    left = summed_copies(exchange(left, XY), near)
    left = summed_copies(exchange(left, "zl"), far)
    left = summed_copies(exchange(left, "zh"), outer)
    own = exchange(left, XY)
    other = lax.ppermute(own, "c", [(0, 1), (1, 0)])

    inner = exchange(inner_products(place, own, columns, 2 * near), ("zl", "c"))
    right = feedback_right(half, own, feedback, 4, None)
    right, gram = feedback_right(1 - half, other, feedback, 4, right)
    inverse = inverse_factor(gram)
    right = add_grads(inner, grads_out, right, outer)
    right = summed_copies(exchange(right, XY), outer)
    right = exchange(right, XY)
    decompressed, right = finish(index_of(XY), half, inverse, own, other, right, width)
    return decompressed, right.T


def solution(mesh):
    outer, tp = mesh.shape["outer"], mesh.shape["tp"]
    across = 4 if outer == 16 else 2
    near = 4 if tp == 32 else 2
    names = ("x", "y", "zh", "zl", "c")
    shape = (outer // across, across, tp // (2 * near), near, 2)
    split_mesh = Mesh(mesh.devices.reshape(shape), names)
    z = ("zh", "zl", "c")
    return jax.shard_map(
        per_device,
        mesh=split_mesh,
        in_specs=(P(XY, z), P(XY, z), P(XY, z), P(z, None)),
        out_specs=(P(XY, z), P(z, None)),
        check_vma=False,
    )
```

```python
import jax
import jax.numpy as jnp
from jax import lax
from jax.experimental import pallas as pl
from jax.experimental.pallas import tpu as pltpu
from jax.sharding import Mesh
from jax.sharding import PartitionSpec as P

F32 = jnp.float32
BF16 = jnp.bfloat16
LANES = 128
XY = ("x", "y")
FAST = dict(preferred_element_type=F32)
FULL = dict(preferred_element_type=F32, precision=lax.Precision.HIGHEST)


def nn(a, b, kind=FAST):
    return lax.dot_general(a, b, (((1,), (0,)), ((), ())), **kind)


def nt(a, b, kind=FAST):
    return lax.dot_general(a, b, (((1,), (1,)), ((), ())), **kind)


def tn(a, b, kind=FAST):
    return lax.dot_general(a, b, (((0,), (0,)), ((), ())), **kind)


def pieces(value):
    high = value.astype(BF16)
    rest = value - high.astype(F32)
    middle = rest.astype(BF16)
    low = (rest - middle.astype(F32)).astype(BF16)
    return jnp.concatenate([high, middle, low], axis=0)


def folded(stacked):
    third = stacked.shape[0] // 3
    return stacked[:third] + (stacked[third : 2 * third] + stacked[2 * third :])


PARAMS = pltpu.CompilerParams(vmem_limit_bytes=16 * 1024 * 1024)


def cost(flops, count):
    return pl.CostEstimate(flops=flops, bytes_accessed=count, transcendentals=0)


def kept_and_given(odd, value):
    half = value.shape[0] // 2
    first, second = value[:half], value[half:]
    return jnp.where(odd, second, first), jnp.where(odd, first, second)


def joined(odd, own, other):
    return jnp.concatenate([jnp.where(odd, other, own), jnp.where(odd, own, other)], axis=0)


def whole_specs(count):
    scalar = pl.BlockSpec(memory_space=pltpu.SMEM)
    return [scalar] + [pl.BlockSpec(memory_space=pltpu.VMEM)] * count


def added_copies(one, two, copies):
    def kernel(one_ref, two_ref, out_ref):
        total = one_ref[...] + two_ref[...]
        for i in range(copies):
            out_ref[i] = total

    return pl.pallas_call(
        kernel,
        out_shape=jax.ShapeDtypeStruct((copies,) + one.shape, F32),
        cost_estimate=cost(one.size, 4 * one.size * (2 + copies)),
        compiler_params=PARAMS,
        name="added_copies",
    )(one, two)


def fetched(feed_ref, held, sems):
    rows = held.shape[0] // sems.shape[0]
    copies = []
    for i in range(sems.shape[0]):
        part = pl.ds(i * rows, rows)
        copies.append(pltpu.make_async_copy(feed_ref.at[part], held.at[part], sems.at[i]))
        copies[-1].start()
    return copies


def left_products(half, start_right, grads, feedback, chunks):
    rows, width = feedback.shape
    rank, tokens = start_right.shape[0], grads.shape[0]
    pairs = rows // (2 * LANES * chunks)

    def kernel(half_ref, start_ref, grads_ref, feed_ref, *refs):
        keep_ref, give_ref, own_ref, other_ref, held, sems, start, held_grads, few = refs
        first = [
            pltpu.make_async_copy(start_ref, start, few.at[0]),
            pltpu.make_async_copy(grads_ref, held_grads, few.at[1]),
        ]
        for copy in first:
            copy.start()
        copies = fetched(feed_ref, held, sems)
        odd = half_ref[0] == 1
        first[0].wait()
        split = pieces(start[...])
        first[1].wait()
        keep_ref[...], give_ref[...] = kept_and_given(odd, folded(nt(split, held_grads[...])))
        for k in range(chunks):
            copies[k].wait()
            part = held[k * (rows // chunks) : (k + 1) * (rows // chunks)]
            result = folded(nt(split, part))
            for i in range(pairs):
                even_rows = result[:, 2 * i * LANES : (2 * i + 1) * LANES]
                odd_rows = result[:, (2 * i + 1) * LANES : (2 * i + 2) * LANES]
                own_ref[k * pairs + i] = jnp.where(odd, odd_rows, even_rows)
                other_ref[k * pairs + i] = jnp.where(odd, even_rows, odd_rows)

    small = jax.ShapeDtypeStruct((rank // 2, tokens), F32)
    large = jax.ShapeDtypeStruct((rows // (2 * LANES), rank, LANES), F32)
    return pl.pallas_call(
        kernel,
        in_specs=whole_specs(0) + [pl.BlockSpec(memory_space=pltpu.HBM)] * 3,
        out_shape=(small, small, large, large),
        scratch_shapes=[
            pltpu.VMEM(feedback.shape, BF16),
            pltpu.SemaphoreType.DMA((chunks,)),
            pltpu.VMEM(start_right.shape, F32),
            pltpu.VMEM(grads.shape, BF16),
            pltpu.SemaphoreType.DMA((2,)),
        ],
        cost_estimate=cost(6 * rank * width * rows, 2 * feedback.size + 4 * rows * rank),
        compiler_params=PARAMS,
        name="left_products",
    )(half, start_right, grads, feedback)


def add_activations(place, inner, columns, own, other):
    near_size, tokens = len(columns), columns[0].shape[0]
    blocks, rank, _ = own.shape

    def kernel(place_ref, inner_ref, inner_other_ref, own_ref, other_ref, *refs):
        column_refs, out_ref = refs[:-1], refs[-1]
        for i in range(blocks):
            out_ref[i] = own_ref[i] + other_ref[i]
        total = joined(place_ref[2] == 1, inner_ref[...], inner_other_ref[...])
        across = jnp.concatenate([ref[...] for ref in column_refs], axis=1)
        extra = folded(nn(pieces(total), across))
        for i in range(near_size):
            block = place_ref[0] * near_size + lax.rem(place_ref[1] + i, near_size)
            out_ref[block] = out_ref[block] + extra[:, i * LANES : (i + 1) * LANES]

    return pl.pallas_call(
        kernel,
        in_specs=whole_specs(4 + near_size),
        out_shape=jax.ShapeDtypeStruct(own.shape, F32),
        cost_estimate=cost(24 * rank * tokens * LANES, 12 * own.size),
        compiler_params=PARAMS,
        name="add_activations",
    )(place, *inner, own, other, *columns)


def summed_copies(shares, copies):
    ways, rows, lanes = shares.shape

    def kernel(shares_ref, out_ref):
        total = shares_ref[0]
        for i in range(1, ways):
            total = total + shares_ref[i]
        for i in range(copies):
            out_ref[i] = total

    return pl.pallas_call(
        kernel,
        out_shape=jax.ShapeDtypeStruct((copies, rows, lanes), F32),
        cost_estimate=cost(shares.size, 4 * shares.size),
        compiler_params=PARAMS,
        name="summed_copies",
    )(shares)


def right_products(half, own, other, gathered, feedback, grads, chunks, parts):
    blocks, rank, _ = own.shape
    rows, width = feedback.shape
    tokens = grads.shape[0]
    pairs = blocks // chunks
    split_rows = rank * width // (256 * parts)
    across = width // 256

    def kernel(
        half_ref, own_ref, other_ref, grads_ref, act_ref, feed_ref, out_ref, gram_ref, held, sems, act, act_sems
    ):
        act_copies = fetched(act_ref, act, act_sems)
        copies = fetched(feed_ref, held, sems)
        odd = half_ref[0] == 1
        right = jnp.zeros((rank, width), F32)
        inner = jnp.zeros((rank, tokens), F32)
        square = jnp.zeros((rank, 3 * rank), F32)
        for k in range(chunks):
            row_blocks = []
            for i in range(k * pairs, (k + 1) * pairs):
                row_blocks.append(jnp.where(odd, other_ref[i], own_ref[i]))
                row_blocks.append(jnp.where(odd, own_ref[i], other_ref[i]))
            split = pieces(jnp.concatenate(row_blocks, axis=1))
            square = square + folded(nt(split, split))
            act_copies[k].wait()
            columns = [act[i] for i in range(2 * k * pairs, 2 * (k + 1) * pairs)]
            inner = inner + folded(nt(split, jnp.concatenate(columns, axis=1)))
            copies[k].wait()
            part = held[k * (rows // chunks) : (k + 1) * (rows // chunks)]
            right = right + folded(nn(split, part))
        right = right + folded(nn(pieces(inner), grads_ref[...]))
        for i in range(parts):
            down, over = i // across * split_rows, i % across * 256
            out_ref[i] = right[down : down + split_rows, over : over + 256]
        gram_ref[...] = square[:, :rank] + square[:, rank : 2 * rank] + square[:, 2 * rank :]

    return pl.pallas_call(
        kernel,
        in_specs=whole_specs(3) + [pl.BlockSpec(memory_space=pltpu.HBM)] * 2,
        out_shape=(
            jax.ShapeDtypeStruct((parts, split_rows, 256), F32),
            jax.ShapeDtypeStruct((rank, rank), F32),
        ),
        scratch_shapes=[
            pltpu.VMEM(feedback.shape, BF16),
            pltpu.SemaphoreType.DMA((chunks,)),
            pltpu.VMEM(gathered.shape, BF16),
            pltpu.SemaphoreType.DMA((chunks,)),
        ],
        cost_estimate=cost(6 * rank * rows * (width + 3 * rank), 2 * feedback.size),
        compiler_params=PARAMS,
        name="right_products",
    )(half, own, other, grads, gathered, feedback)


def inverse_factor(gram):
    rank = gram.shape[0]

    def kernel(gram_ref, out_ref):
        row = lax.broadcasted_iota(jnp.int32, (rank, rank), 0)
        col = lax.broadcasted_iota(jnp.int32, (rank, rank), 1)
        work = jnp.concatenate([gram_ref[...], (row == col).astype(F32)], axis=1)
        index = lax.broadcasted_iota(jnp.int32, (rank, 1), 0)
        for k in range(rank):
            low = k // 8 * 8
            pivot_row = work[k : k + 1]
            scale = 1.0 / work[k : k + 1, k : k + 1]
            part = work[low:]
            factor = jnp.where(index[low:] > k, part[:, k : k + 1] * scale, 0.0)
            part = part - factor * pivot_row
            work = part if low == 0 else jnp.concatenate([work[:low], part], axis=0)
        diagonal = jnp.sum(jnp.where(row == col, work[:, :rank], 0.0), axis=1, keepdims=True)
        out_ref[...] = work[:, rank:] / jnp.sqrt(diagonal)

    return pl.pallas_call(
        kernel,
        out_shape=jax.ShapeDtypeStruct((rank, rank), F32),
        cost_estimate=cost(2 * rank * rank * rank * 8, 8 * rank * rank),
        compiler_params=PARAMS,
        name="inverse_factor",
    )(gram)


def finish(place, half, inverse, own, other, gathered, width):
    rank = inverse.shape[0]
    parts = gathered.shape[0]
    across = width // 256
    slab = 2 * LANES

    def kernel(place_ref, half_ref, inverse_ref, own_ref, other_ref, gathered_ref, dec_ref, right_ref):
        across_rows = [
            jnp.concatenate([gathered_ref[i + j] for j in range(across)], axis=1)
            for i in range(0, parts, across)
        ]
        right = nn(inverse_ref[...], jnp.concatenate(across_rows, axis=0), FULL)
        right_ref[...] = right
        odd = half_ref[0] == 1
        even_rows = jnp.where(odd, other_ref[0], own_ref[0])
        odd_rows = jnp.where(odd, own_ref[0], other_ref[0])
        basis = nn(inverse_ref[...], jnp.concatenate([even_rows, odd_rows], axis=1), FULL)
        dec_ref[...] = tn(basis, right, FULL).astype(BF16)

    block = pl.BlockSpec((1, rank, LANES), lambda i, place, half: (place[0], 0, 0))
    return pl.pallas_call(
        kernel,
        grid_spec=pltpu.PrefetchScalarGridSpec(
            num_scalar_prefetch=2,
            grid=(1,),
            in_specs=[
                pl.BlockSpec(inverse.shape, lambda i, place, half: (0, 0)),
                block,
                block,
                pl.BlockSpec(gathered.shape, lambda i, place, half: (0, 0, 0)),
            ],
            out_specs=[
                pl.BlockSpec((slab, width), lambda i, place, half: (0, 0)),
                pl.BlockSpec((rank, width), lambda i, place, half: (0, 0)),
            ],
        ),
        out_shape=(
            jax.ShapeDtypeStruct((slab, width), BF16),
            jax.ShapeDtypeStruct((rank, width), F32),
        ),
        cost_estimate=cost(12 * rank * slab * width, 4 * gathered.size),
        compiler_params=PARAMS,
        name="finish",
    )(place, half, inverse, own, other, gathered)


def exchange(value, axes):
    return lax.all_to_all(value, axes, 0, 0, tiled=True)


def in_hbm(value):
    return pltpu.with_memory_space_constraint(value, pltpu.HBM)


def index_of(axes):
    return lax.axis_index(axes).astype(jnp.int32).reshape(1)


def swapped(value):
    return lax.ppermute(value, "c", [(0, 1), (1, 0)])


def per_device(activations, grads_out, feedback, start_right):
    width = grads_out.shape[1]
    far, near = lax.axis_size("zh"), lax.axis_size("zl")
    outer = lax.axis_size(XY)
    half = index_of("c")
    place = jnp.concatenate([index_of("zh"), index_of("zl"), half])
    feedback = in_hbm(feedback)

    gathered = lax.all_gather(activations, ("zh", "zl", "c"), axis=0)
    columns = [activations] + [
        lax.ppermute(activations, "zl", [((i + j) % near, i) for i in range(near)])
        for j in range(1, near)
    ]
    keep, give, own, other = left_products(
        half, in_hbm(start_right.T), in_hbm(grads_out), feedback, 4
    )
    inner = added_copies(keep, swapped(give), far)
    inner = summed_copies(exchange(inner, "zh"), 1)[0]
    left = add_activations(place, (inner, swapped(inner)), columns, own, swapped(other))

    left = summed_copies(exchange(left, XY), near)
    left = summed_copies(exchange(left, "zl"), far)
    left = summed_copies(exchange(left, "zh"), outer)
    own = exchange(left, XY)
    other = swapped(own)

    right, gram = right_products(half, own, other, in_hbm(gathered), feedback, grads_out, 4, outer)
    inverse = inverse_factor(gram)
    right = summed_copies(exchange(right, XY), outer)
    right = exchange(right, XY)
    decompressed, right = finish(index_of(XY), half, inverse, own, other, right, width)
    return decompressed, right.T


def solution(mesh):
    outer, tp = mesh.shape["outer"], mesh.shape["tp"]
    across = 4 if outer == 16 else 2
    near = 4 if tp == 32 else 2
    names = ("x", "y", "zh", "zl", "c")
    shape = (outer // across, across, tp // (2 * near), near, 2)
    split_mesh = Mesh(mesh.devices.reshape(shape), names)
    z = ("zh", "zl", "c")
    return jax.shard_map(
        per_device,
        mesh=split_mesh,
        in_specs=(P(XY, z), P(XY, z), P(XY, z), P(z, None)),
        out_specs=(P(XY, z), P(z, None)),
        check_vma=False,
    )
```

```python
import jax
import jax.numpy as jnp
from jax import lax
from jax.experimental import pallas as pl
from jax.experimental.pallas import tpu as pltpu
from jax.sharding import Mesh
from jax.sharding import PartitionSpec as P

F32 = jnp.float32
BF16 = jnp.bfloat16
LANES = 128
XY = ("x", "y")
FAST = dict(preferred_element_type=F32)
FULL = dict(preferred_element_type=F32, precision=lax.Precision.HIGHEST)


def nn(a, b, kind=FAST):
    return lax.dot_general(a, b, (((1,), (0,)), ((), ())), **kind)


def nt(a, b, kind=FAST):
    return lax.dot_general(a, b, (((1,), (1,)), ((), ())), **kind)


def tn(a, b, kind=FAST):
    return lax.dot_general(a, b, (((0,), (0,)), ((), ())), **kind)


def pieces(value):
    high = value.astype(BF16)
    rest = value - high.astype(F32)
    middle = rest.astype(BF16)
    low = (rest - middle.astype(F32)).astype(BF16)
    return jnp.concatenate([high, middle, low], axis=0)


def folded(stacked):
    third = stacked.shape[0] // 3
    return stacked[:third] + (stacked[third : 2 * third] + stacked[2 * third :])


PARAMS = pltpu.CompilerParams(vmem_limit_bytes=16 * 1024 * 1024)


def cost(flops, count):
    return pl.CostEstimate(flops=flops, bytes_accessed=count, transcendentals=0)


def whole_specs(count):
    scalar = pl.BlockSpec(memory_space=pltpu.SMEM)
    return [scalar] + [pl.BlockSpec(memory_space=pltpu.VMEM)] * count


def copied(value, copies):
    def kernel(value_ref, out_ref, sems):
        started = [
            pltpu.make_async_copy(value_ref, out_ref.at[i], sems.at[i]) for i in range(copies)
        ]
        for copy in started:
            copy.start()
        for copy in started:
            copy.wait()

    return pl.pallas_call(
        kernel,
        in_specs=[pl.BlockSpec(memory_space=pltpu.HBM)],
        out_shape=jax.ShapeDtypeStruct((copies,) + value.shape, value.dtype),
        scratch_shapes=[pltpu.SemaphoreType.DMA((copies,))],
        cost_estimate=cost(0, 2 * value.size * (1 + copies)),
        compiler_params=PARAMS,
        name="copied",
    )(value)


def added_copies(one, two, copies):
    def kernel(one_ref, two_ref, out_ref):
        total = one_ref[...] + two_ref[...]
        for i in range(copies):
            out_ref[i] = total

    return pl.pallas_call(
        kernel,
        out_shape=jax.ShapeDtypeStruct((copies,) + one.shape, F32),
        cost_estimate=cost(one.size, 4 * one.size * (2 + copies)),
        compiler_params=PARAMS,
        name="added_copies",
    )(one, two)


def added(one, two):
    def kernel(one_ref, two_ref, out_ref):
        out_ref[...] = one_ref[...] + two_ref[...]

    return pl.pallas_call(
        kernel,
        out_shape=jax.ShapeDtypeStruct(one.shape, F32),
        cost_estimate=cost(one.size, 12 * one.size),
        compiler_params=PARAMS,
        name="added",
    )(one, two)


def fetched(feed_ref, held, sems):
    rows = held.shape[0] // sems.shape[0]
    copies = []
    for i in range(sems.shape[0]):
        part = pl.ds(i * rows, rows)
        copies.append(pltpu.make_async_copy(feed_ref.at[part], held.at[part], sems.at[i]))
        copies[-1].start()
    return copies


def left_products(half, start_right, grads, feedback, chunks):
    rows, width = feedback.shape
    rank, tokens = start_right.shape[0], grads.shape[0]
    pairs = rows // (2 * LANES * chunks)

    def kernel(half_ref, start_ref, grads_ref, feed_ref, *refs):
        inner_ref, own_ref, other_ref, held, sems, start, held_grads, few = refs
        first = [
            pltpu.make_async_copy(start_ref, start, few.at[0]),
            pltpu.make_async_copy(grads_ref, held_grads, few.at[1]),
        ]
        for copy in first:
            copy.start()
        copies = fetched(feed_ref, held, sems)
        odd = half_ref[0] == 1
        first[0].wait()
        split = pieces(start[...])
        first[1].wait()
        inner_ref[...] = folded(nt(split, held_grads[...]))
        for k in range(chunks):
            copies[k].wait()
            part = held[k * (rows // chunks) : (k + 1) * (rows // chunks)]
            result = folded(nt(split, part))
            for i in range(pairs):
                even_rows = result[:, 2 * i * LANES : (2 * i + 1) * LANES]
                odd_rows = result[:, (2 * i + 1) * LANES : (2 * i + 2) * LANES]
                own_ref[k * pairs + i] = jnp.where(odd, odd_rows, even_rows)
                other_ref[k * pairs + i] = jnp.where(odd, even_rows, odd_rows)

    small = jax.ShapeDtypeStruct((rank, tokens), F32)
    large = jax.ShapeDtypeStruct((rows // (2 * LANES), rank, LANES), F32)
    return pl.pallas_call(
        kernel,
        in_specs=whole_specs(0) + [pl.BlockSpec(memory_space=pltpu.HBM)] * 3,
        out_shape=(small, large, large),
        scratch_shapes=[
            pltpu.VMEM(feedback.shape, BF16),
            pltpu.SemaphoreType.DMA((chunks,)),
            pltpu.VMEM(start_right.shape, F32),
            pltpu.VMEM(grads.shape, BF16),
            pltpu.SemaphoreType.DMA((2,)),
        ],
        cost_estimate=cost(6 * rank * width * rows, 2 * feedback.size + 4 * rows * rank),
        compiler_params=PARAMS,
        name="left_products",
    )(half, start_right, grads, feedback)


def add_activations(place, inner, columns, own, other):
    far_size, tokens, _ = columns.shape
    blocks, rank, _ = own.shape

    def kernel(place_ref, columns_ref, own_ref, other_ref, *refs):
        inner_refs, out_ref = refs[:-1], refs[-1]
        for i in range(blocks):
            out_ref[i] = own_ref[i] + other_ref[i]
        total = inner_refs[0][...]
        for ref in inner_refs[1:]:
            total = total + ref[...]
        across = jnp.concatenate([columns_ref[i] for i in range(far_size)], axis=1)
        extra = folded(nn(pieces(total), across))
        for i in range(far_size):
            block = i * (blocks // far_size) + place_ref[0]
            out_ref[block] = out_ref[block] + extra[:, i * LANES : (i + 1) * LANES]

    return pl.pallas_call(
        kernel,
        in_specs=whole_specs(3 + len(inner)),
        out_shape=jax.ShapeDtypeStruct(own.shape, F32),
        cost_estimate=cost(24 * rank * tokens * LANES, 12 * own.size),
        compiler_params=PARAMS,
        name="add_activations",
    )(place, columns, own, other, *inner)


def summed_copies(shares, copies):
    ways, rows, lanes = shares.shape

    def kernel(shares_ref, out_ref):
        total = shares_ref[0]
        for i in range(1, ways):
            total = total + shares_ref[i]
        for i in range(copies):
            out_ref[i] = total

    return pl.pallas_call(
        kernel,
        out_shape=jax.ShapeDtypeStruct((copies, rows, lanes), F32),
        cost_estimate=cost(shares.size, 4 * shares.size),
        compiler_params=PARAMS,
        name="summed_copies",
    )(shares)


def inner_products(near, left, columns):
    blocks, rank, _ = left.shape
    far_size, tokens, _ = columns.shape

    def kernel(near_ref, left_ref, columns_ref, out_ref):
        rows = [left_ref[i * (blocks // far_size) + near_ref[0]] for i in range(far_size)]
        across = jnp.concatenate([columns_ref[i] for i in range(far_size)], axis=1)
        out_ref[...] = folded(nt(pieces(jnp.concatenate(rows, axis=1)), across))

    return pl.pallas_call(
        kernel,
        in_specs=whole_specs(2),
        out_shape=jax.ShapeDtypeStruct((rank, tokens), F32),
        cost_estimate=cost(6 * rank * tokens * far_size * LANES, 2 * columns.size),
        compiler_params=PARAMS,
        name="inner_products",
    )(near, left, columns)


def feedback_right(half, own, other, feedback, chunks):
    blocks, rank, _ = own.shape
    rows, width = feedback.shape
    pairs = blocks // chunks

    def kernel(half_ref, own_ref, other_ref, feed_ref, out_ref, gram_ref, held, sems):
        copies = fetched(feed_ref, held, sems)
        odd = half_ref[0] == 1
        right = jnp.zeros((rank, width), F32)
        square = jnp.zeros((rank, 3 * rank), F32)
        for k in range(chunks):
            row_blocks = []
            for i in range(k * pairs, (k + 1) * pairs):
                row_blocks.append(jnp.where(odd, other_ref[i], own_ref[i]))
                row_blocks.append(jnp.where(odd, own_ref[i], other_ref[i]))
            split = pieces(jnp.concatenate(row_blocks, axis=1))
            square = square + folded(nt(split, split))
            copies[k].wait()
            part = held[k * (rows // chunks) : (k + 1) * (rows // chunks)]
            right = right + folded(nn(split, part))
        out_ref[...] = right
        gram_ref[...] = square[:, :rank] + square[:, rank : 2 * rank] + square[:, 2 * rank :]

    return pl.pallas_call(
        kernel,
        in_specs=whole_specs(2) + [pl.BlockSpec(memory_space=pltpu.HBM)],
        out_shape=(
            jax.ShapeDtypeStruct((rank, width), F32),
            jax.ShapeDtypeStruct((rank, rank), F32),
        ),
        scratch_shapes=[pltpu.VMEM(feedback.shape, BF16), pltpu.SemaphoreType.DMA((chunks,))],
        cost_estimate=cost(6 * rank * rows * (width + 3 * rank), 2 * feedback.size),
        compiler_params=PARAMS,
        name="feedback_right",
    )(half, own, other, feedback)


def add_grads(shares, grads, partial, parts):
    ways, rank, tokens = shares.shape
    width = grads.shape[1]
    split_rows = rank * width // (256 * parts)
    across = width // 256

    def kernel(shares_ref, grads_ref, partial_ref, out_ref):
        inner = shares_ref[0]
        for i in range(1, ways):
            inner = inner + shares_ref[i]
        total = partial_ref[...] + folded(nn(pieces(inner), grads_ref[...]))
        for i in range(parts):
            down, over = i // across * split_rows, i % across * 256
            out_ref[i] = total[down : down + split_rows, over : over + 256]

    return pl.pallas_call(
        kernel,
        out_shape=jax.ShapeDtypeStruct((parts, split_rows, 256), F32),
        cost_estimate=cost(6 * rank * tokens * width, 4 * shares.size + 2 * grads.size),
        compiler_params=PARAMS,
        name="add_grads",
    )(shares, grads, partial)


def inverse_factor(gram):
    rank = gram.shape[0]

    def kernel(gram_ref, out_ref):
        row = lax.broadcasted_iota(jnp.int32, (rank, rank), 0)
        col = lax.broadcasted_iota(jnp.int32, (rank, rank), 1)
        work = jnp.concatenate([gram_ref[...], (row == col).astype(F32)], axis=1)
        index = lax.broadcasted_iota(jnp.int32, (rank, 1), 0)
        for k in range(rank):
            low = k // 8 * 8
            pivot_row = work[k : k + 1]
            scale = 1.0 / work[k : k + 1, k : k + 1]
            part = work[low:]
            factor = jnp.where(index[low:] > k, part[:, k : k + 1] * scale, 0.0)
            part = part - factor * pivot_row
            work = part if low == 0 else jnp.concatenate([work[:low], part], axis=0)
        diagonal = jnp.sum(jnp.where(row == col, work[:, :rank], 0.0), axis=1, keepdims=True)
        out_ref[...] = work[:, rank:] / jnp.sqrt(diagonal)

    return pl.pallas_call(
        kernel,
        out_shape=jax.ShapeDtypeStruct((rank, rank), F32),
        cost_estimate=cost(2 * rank * rank * rank * 8, 8 * rank * rank),
        compiler_params=PARAMS,
        name="inverse_factor",
    )(gram)


def finish(place, half, inverse, own, other, gathered, width):
    rank = inverse.shape[0]
    parts = gathered.shape[0]
    across = width // 256
    slab = 2 * LANES

    def kernel(place_ref, half_ref, inverse_ref, own_ref, other_ref, gathered_ref, dec_ref, right_ref):
        across_rows = [
            jnp.concatenate([gathered_ref[i + j] for j in range(across)], axis=1)
            for i in range(0, parts, across)
        ]
        right = nn(inverse_ref[...], jnp.concatenate(across_rows, axis=0), FULL)
        right_ref[...] = right
        odd = half_ref[0] == 1
        even_rows = jnp.where(odd, other_ref[0], own_ref[0])
        odd_rows = jnp.where(odd, own_ref[0], other_ref[0])
        basis = nn(inverse_ref[...], jnp.concatenate([even_rows, odd_rows], axis=1), FULL)
        dec_ref[...] = tn(basis, right, FULL).astype(BF16)

    block = pl.BlockSpec((1, rank, LANES), lambda i, place, half: (place[0], 0, 0))
    return pl.pallas_call(
        kernel,
        grid_spec=pltpu.PrefetchScalarGridSpec(
            num_scalar_prefetch=2,
            grid=(1,),
            in_specs=[
                pl.BlockSpec(inverse.shape, lambda i, place, half: (0, 0)),
                block,
                block,
                pl.BlockSpec(gathered.shape, lambda i, place, half: (0, 0, 0)),
            ],
            out_specs=[
                pl.BlockSpec((slab, width), lambda i, place, half: (0, 0)),
                pl.BlockSpec((rank, width), lambda i, place, half: (0, 0)),
            ],
        ),
        out_shape=(
            jax.ShapeDtypeStruct((slab, width), BF16),
            jax.ShapeDtypeStruct((rank, width), F32),
        ),
        cost_estimate=cost(12 * rank * slab * width, 4 * gathered.size),
        compiler_params=PARAMS,
        name="finish",
    )(place, half, inverse, own, other, gathered)


def exchange(value, axes):
    return lax.all_to_all(value, axes, 0, 0, tiled=True)


def in_hbm(value):
    return pltpu.with_memory_space_constraint(value, pltpu.HBM)


def index_of(axes):
    return lax.axis_index(axes).astype(jnp.int32).reshape(1)


def swapped(value):
    return lax.ppermute(value, "c", [(0, 1), (1, 0)])


def per_device(activations, grads_out, feedback, start_right):
    width = grads_out.shape[1]
    far, near = lax.axis_size("zh"), lax.axis_size("zl")
    outer = lax.axis_size(XY)
    half = index_of("c")
    feedback = in_hbm(feedback)

    columns = exchange(copied(in_hbm(activations), far), "zh")
    inner, own, other = left_products(
        half, in_hbm(start_right.T), in_hbm(grads_out), feedback, 4
    )
    inner = added(inner, swapped(inner))
    inner = [inner] + [
        lax.ppermute(inner, "zl", [((i + j) % near, i) for i in range(near)])
        for j in range(1, near)
    ]
    left = add_activations(index_of("zl"), inner, columns, own, swapped(other))

    left = summed_copies(exchange(left, XY), near)
    left = summed_copies(exchange(left, "zl"), far)
    left = summed_copies(exchange(left, "zh"), outer)
    own = exchange(left, XY)
    other = swapped(own)

    inner = inner_products(index_of("zl"), own, columns)
    inner = exchange(added_copies(inner, swapped(inner), near), "zl")
    right, gram = feedback_right(half, own, other, feedback, 4)
    right = add_grads(inner, grads_out, right, outer)
    inverse = inverse_factor(gram)
    right = summed_copies(exchange(right, XY), outer)
    right = exchange(right, XY)
    decompressed, right = finish(index_of(XY), half, inverse, own, other, right, width)
    return decompressed, right.T


def solution(mesh):
    outer, tp = mesh.shape["outer"], mesh.shape["tp"]
    across = 4 if outer == 16 else 2
    near = 4 if tp == 32 else 2
    names = ("x", "y", "zh", "zl", "c")
    shape = (outer // across, across, tp // (2 * near), near, 2)
    split_mesh = Mesh(mesh.devices.reshape(shape), names)
    z = ("zh", "zl", "c")
    return jax.shard_map(
        per_device,
        mesh=split_mesh,
        in_specs=(P(XY, z), P(XY, z), P(XY, z), P(z, None)),
        out_specs=(P(XY, z), P(z, None)),
        check_vma=False,
    )
```

```python
import jax
import jax.numpy as jnp
from jax import lax
from jax.experimental import pallas as pl
from jax.experimental.pallas import tpu as pltpu
from jax.sharding import Mesh
from jax.sharding import PartitionSpec as P

F32 = jnp.float32
BF16 = jnp.bfloat16
LANES = 128
XY = ("x", "y")
FAST = dict(preferred_element_type=F32)
FULL = dict(preferred_element_type=F32, precision=lax.Precision.HIGHEST)


def nn(a, b, kind=FAST):
    return lax.dot_general(a, b, (((1,), (0,)), ((), ())), **kind)


def nt(a, b, kind=FAST):
    return lax.dot_general(a, b, (((1,), (1,)), ((), ())), **kind)


def tn(a, b, kind=FAST):
    return lax.dot_general(a, b, (((0,), (0,)), ((), ())), **kind)


def pieces(value):
    high = value.astype(BF16)
    rest = value - high.astype(F32)
    middle = rest.astype(BF16)
    low = (rest - middle.astype(F32)).astype(BF16)
    return jnp.concatenate([high, middle, low], axis=0)


def folded(stacked):
    third = stacked.shape[0] // 3
    return stacked[:third] + (stacked[third : 2 * third] + stacked[2 * third :])


PARAMS = pltpu.CompilerParams(vmem_limit_bytes=16 * 1024 * 1024)


def cost(flops, count):
    return pl.CostEstimate(flops=flops, bytes_accessed=count, transcendentals=0)


def joined(odd, own, other):
    return jnp.concatenate([jnp.where(odd, other, own), jnp.where(odd, own, other)], axis=0)


def whole_specs(count):
    scalar = pl.BlockSpec(memory_space=pltpu.SMEM)
    return [scalar] + [pl.BlockSpec(memory_space=pltpu.VMEM)] * count


def added_tail(one, two):
    blocks = two.shape[0]

    def kernel(one_ref, two_ref, out_ref):
        tail = jnp.concatenate([two_ref[blocks - 2], two_ref[blocks - 1]], axis=1)
        out_ref[...] = one_ref[...] + tail

    return pl.pallas_call(
        kernel,
        out_shape=jax.ShapeDtypeStruct(one.shape, F32),
        cost_estimate=cost(one.size, 12 * one.size),
        compiler_params=PARAMS,
        name="added_tail",
    )(one, two)


def fetched(feed_ref, held, sems):
    rows = held.shape[0] // sems.shape[0]
    copies = []
    for i in range(sems.shape[0]):
        part = pl.ds(i * rows, rows)
        copies.append(pltpu.make_async_copy(feed_ref.at[part], held.at[part], sems.at[i]))
        copies[-1].start()
    return copies


def left_products(half, start_right, grads, activations, feedback, chunks, copies_wanted):
    rows, width = feedback.shape
    rank, tokens = start_right.shape[0], grads.shape[0]
    pairs = rows // (2 * LANES * chunks)

    def kernel(half_ref, start_ref, grads_ref, act_ref, feed_ref, *refs):
        inner_ref, own_ref, other_ref, copies_ref, held, sems, start, held_grads, few = refs
        first = [
            pltpu.make_async_copy(start_ref, start, few.at[0]),
            pltpu.make_async_copy(grads_ref, held_grads, few.at[1]),
        ] + [
            pltpu.make_async_copy(act_ref, copies_ref.at[i], few.at[2 + i])
            for i in range(copies_wanted)
        ]
        for copy in first:
            copy.start()
        copies = fetched(feed_ref, held, sems)
        odd = half_ref[0] == 1
        first[0].wait()
        split = pieces(start[...])
        first[1].wait()
        inner = folded(nt(split, held_grads[...]))
        inner_ref[...] = inner
        other_ref[chunks * pairs] = inner[:, :LANES]
        other_ref[chunks * pairs + 1] = inner[:, LANES:]
        for k in range(chunks):
            copies[k].wait()
            part = held[k * (rows // chunks) : (k + 1) * (rows // chunks)]
            result = folded(nt(split, part))
            for i in range(pairs):
                even_rows = result[:, 2 * i * LANES : (2 * i + 1) * LANES]
                odd_rows = result[:, (2 * i + 1) * LANES : (2 * i + 2) * LANES]
                own_ref[k * pairs + i] = jnp.where(odd, odd_rows, even_rows)
                other_ref[k * pairs + i] = jnp.where(odd, even_rows, odd_rows)
        for copy in first[2:]:
            copy.wait()

    small = jax.ShapeDtypeStruct((rank, tokens), F32)
    large = jax.ShapeDtypeStruct((rows // (2 * LANES), rank, LANES), F32)
    longer = jax.ShapeDtypeStruct((rows // (2 * LANES) + 2, rank, LANES), F32)
    repeated = jax.ShapeDtypeStruct((copies_wanted,) + activations.shape, BF16)
    return pl.pallas_call(
        kernel,
        in_specs=whole_specs(0) + [pl.BlockSpec(memory_space=pltpu.HBM)] * 4,
        out_shape=(small, large, longer, repeated),
        scratch_shapes=[
            pltpu.VMEM(feedback.shape, BF16),
            pltpu.SemaphoreType.DMA((chunks,)),
            pltpu.VMEM(start_right.shape, F32),
            pltpu.VMEM(grads.shape, BF16),
            pltpu.SemaphoreType.DMA((2 + copies_wanted,)),
        ],
        cost_estimate=cost(6 * rank * width * rows, 2 * feedback.size + 4 * rows * rank),
        compiler_params=PARAMS,
        name="left_products",
    )(half, start_right, grads, activations, feedback)


def add_activations(place, inner, columns, own, other):
    far_size, tokens, _ = columns.shape
    blocks, rank, _ = own.shape

    def kernel(place_ref, columns_ref, own_ref, other_ref, *refs):
        inner_refs, out_ref = refs[:-1], refs[-1]
        for i in range(blocks):
            out_ref[i] = own_ref[i] + other_ref[i]
        total = inner_refs[0][...]
        for ref in inner_refs[1:]:
            total = total + ref[...]
        across = jnp.concatenate([columns_ref[i] for i in range(far_size)], axis=1)
        extra = folded(nn(pieces(total), across))
        for i in range(far_size):
            group = (i + far_size // 2) % far_size
            block = group * (blocks // far_size) + place_ref[0]
            out_ref[block] = out_ref[block] + extra[:, i * LANES : (i + 1) * LANES]

    return pl.pallas_call(
        kernel,
        in_specs=whole_specs(3 + len(inner)),
        out_shape=jax.ShapeDtypeStruct(own.shape, F32),
        cost_estimate=cost(24 * rank * tokens * LANES, 12 * own.size),
        compiler_params=PARAMS,
        name="add_activations",
    )(place, columns, own, other, *inner)


def summed_copies(shares, copies):
    ways, rows, lanes = shares.shape

    def kernel(shares_ref, out_ref):
        total = shares_ref[0]
        for i in range(1, ways):
            total = total + shares_ref[i]
        for i in range(copies):
            out_ref[i] = total

    return pl.pallas_call(
        kernel,
        out_shape=jax.ShapeDtypeStruct((copies, rows, lanes), F32),
        cost_estimate=cost(shares.size, 4 * shares.size),
        compiler_params=PARAMS,
        name="summed_copies",
    )(shares)


def inner_products(near, left, columns):
    blocks, rank, _ = left.shape
    far_size, tokens, _ = columns.shape

    def kernel(near_ref, left_ref, columns_ref, out_ref):
        near_size = blocks // far_size
        groups = [(i + far_size // 2) % far_size for i in range(far_size)]
        rows = [left_ref[group * near_size + near_ref[0]] for group in groups]
        across = jnp.concatenate([columns_ref[i] for i in range(far_size)], axis=1)
        result = folded(nt(pieces(jnp.concatenate(rows, axis=1)), across))
        for i in range(near_size):
            out_ref[2 * i] = result[: rank // 2]
            out_ref[2 * i + 1] = result[rank // 2 :]

    return pl.pallas_call(
        kernel,
        in_specs=whole_specs(2),
        out_shape=jax.ShapeDtypeStruct((2 * blocks // far_size, rank // 2, tokens), F32),
        cost_estimate=cost(6 * rank * tokens * far_size * LANES, 2 * columns.size),
        compiler_params=PARAMS,
        name="inner_products",
    )(near, left, columns)


def feedback_right(half, own, other, feedback, chunks):
    blocks, rank, _ = own.shape
    rows, width = feedback.shape
    pairs = blocks // chunks

    def kernel(half_ref, own_ref, other_ref, feed_ref, out_ref, gram_ref, held, sems):
        copies = fetched(feed_ref, held, sems)
        odd = half_ref[0] == 1
        right = jnp.zeros((rank, width), F32)
        square = jnp.zeros((rank, 3 * rank), F32)
        for k in range(chunks):
            row_blocks = []
            for i in range(k * pairs, (k + 1) * pairs):
                row_blocks.append(jnp.where(odd, other_ref[i], own_ref[i]))
                row_blocks.append(jnp.where(odd, own_ref[i], other_ref[i]))
            split = pieces(jnp.concatenate(row_blocks, axis=1))
            square = square + folded(nt(split, split))
            copies[k].wait()
            part = held[k * (rows // chunks) : (k + 1) * (rows // chunks)]
            right = right + folded(nn(split, part))
        out_ref[...] = right
        gram_ref[...] = square[:, :rank] + square[:, rank : 2 * rank] + square[:, 2 * rank :]

    return pl.pallas_call(
        kernel,
        in_specs=whole_specs(2) + [pl.BlockSpec(memory_space=pltpu.HBM)],
        out_shape=(
            jax.ShapeDtypeStruct((rank, width), F32),
            jax.ShapeDtypeStruct((rank, rank), F32),
        ),
        scratch_shapes=[pltpu.VMEM(feedback.shape, BF16), pltpu.SemaphoreType.DMA((chunks,))],
        cost_estimate=cost(6 * rank * rows * (width + 3 * rank), 2 * feedback.size),
        compiler_params=PARAMS,
        name="feedback_right",
    )(half, own, other, feedback)


def add_grads(half, inner, inner_other, grads, partial, parts):
    rank, width = partial.shape
    tokens = grads.shape[0]
    split_rows = rank * width // (256 * parts)
    across = width // 256

    def kernel(half_ref, inner_ref, inner_other_ref, grads_ref, partial_ref, out_ref):
        inner = joined(half_ref[0] == 1, inner_ref[...], inner_other_ref[...])
        total = partial_ref[...] + folded(nn(pieces(inner), grads_ref[...]))
        for i in range(parts):
            down, over = i // across * split_rows, i % across * 256
            out_ref[i] = total[down : down + split_rows, over : over + 256]

    return pl.pallas_call(
        kernel,
        in_specs=whole_specs(4),
        out_shape=jax.ShapeDtypeStruct((parts, split_rows, 256), F32),
        cost_estimate=cost(6 * rank * tokens * width, 8 * inner.size + 2 * grads.size),
        compiler_params=PARAMS,
        name="add_grads",
    )(half, inner, inner_other, grads, partial)


def inverse_factor(gram):
    rank = gram.shape[0]

    def kernel(gram_ref, out_ref):
        row = lax.broadcasted_iota(jnp.int32, (rank, rank), 0)
        col = lax.broadcasted_iota(jnp.int32, (rank, rank), 1)
        work = jnp.concatenate([gram_ref[...], (row == col).astype(F32)], axis=1)
        index = lax.broadcasted_iota(jnp.int32, (rank, 1), 0)
        for k in range(rank):
            low = k // 8 * 8
            pivot_row = work[k : k + 1]
            scale = 1.0 / work[k : k + 1, k : k + 1]
            part = work[low:]
            factor = jnp.where(index[low:] > k, part[:, k : k + 1] * scale, 0.0)
            part = part - factor * pivot_row
            work = part if low == 0 else jnp.concatenate([work[:low], part], axis=0)
        diagonal = jnp.sum(jnp.where(row == col, work[:, :rank], 0.0), axis=1, keepdims=True)
        out_ref[...] = work[:, rank:] / jnp.sqrt(diagonal)

    return pl.pallas_call(
        kernel,
        out_shape=jax.ShapeDtypeStruct((rank, rank), F32),
        cost_estimate=cost(2 * rank * rank * rank * 8, 8 * rank * rank),
        compiler_params=PARAMS,
        name="inverse_factor",
    )(gram)


def finish(place, half, inverse, own, other, gathered, width):
    rank = inverse.shape[0]
    parts = gathered.shape[0]
    across = width // 256
    slab = 2 * LANES

    def kernel(place_ref, half_ref, inverse_ref, own_ref, other_ref, gathered_ref, dec_ref, right_ref):
        across_rows = [
            jnp.concatenate([gathered_ref[i + j] for j in range(across)], axis=1)
            for i in range(0, parts, across)
        ]
        right = nn(inverse_ref[...], jnp.concatenate(across_rows, axis=0), FULL)
        right_ref[...] = right
        odd = half_ref[0] == 1
        even_rows = jnp.where(odd, other_ref[0], own_ref[0])
        odd_rows = jnp.where(odd, own_ref[0], other_ref[0])
        basis = nn(inverse_ref[...], jnp.concatenate([even_rows, odd_rows], axis=1), FULL)
        dec_ref[...] = tn(basis, right, FULL).astype(BF16)

    block = pl.BlockSpec((1, rank, LANES), lambda i, place, half: (place[0], 0, 0))
    return pl.pallas_call(
        kernel,
        grid_spec=pltpu.PrefetchScalarGridSpec(
            num_scalar_prefetch=2,
            grid=(1,),
            in_specs=[
                pl.BlockSpec(inverse.shape, lambda i, place, half: (0, 0)),
                block,
                block,
                pl.BlockSpec(gathered.shape, lambda i, place, half: (0, 0, 0)),
            ],
            out_specs=[
                pl.BlockSpec((slab, width), lambda i, place, half: (0, 0)),
                pl.BlockSpec((rank, width), lambda i, place, half: (0, 0)),
            ],
        ),
        out_shape=(
            jax.ShapeDtypeStruct((slab, width), BF16),
            jax.ShapeDtypeStruct((rank, width), F32),
        ),
        cost_estimate=cost(12 * rank * slab * width, 4 * gathered.size),
        compiler_params=PARAMS,
        name="finish",
    )(place, half, inverse, own, other, gathered)


def exchange(value, axes, first=0):
    size = lax.axis_size(axes)
    order = [(i + first) % size for i in range(size)]
    return lax.all_to_all(value, axes, 0, 0, axis_index_groups=[order], tiled=True)


def in_hbm(value):
    return pltpu.with_memory_space_constraint(value, pltpu.HBM)


def index_of(axes):
    return lax.axis_index(axes).astype(jnp.int32).reshape(1)


def swapped(value):
    return lax.ppermute(value, "c", [(0, 1), (1, 0)])


def per_device(activations, grads_out, feedback, start_right):
    width = grads_out.shape[1]
    far, near = lax.axis_size("zh"), lax.axis_size("zl")
    outer = lax.axis_size(XY)
    half = index_of("c")
    feedback = in_hbm(feedback)

    inner, own, other, columns = left_products(
        half, in_hbm(start_right.T), in_hbm(grads_out), in_hbm(activations), feedback, 4, far
    )
    columns = exchange(columns, "zh", far // 2)
    other = swapped(other)
    inner = added_tail(inner, other)
    inner = [inner] + [
        lax.ppermute(inner, "zl", [((i + j) % near, i) for i in range(near)])
        for j in range(1, near)
    ]
    left = add_activations(index_of("zl"), inner, columns, own, other)

    left = summed_copies(exchange(left, XY), near)
    left = summed_copies(exchange(left, "zl", 1), far)
    left = summed_copies(exchange(left, "zh", far // 2), outer)
    own = exchange(left, XY)
    other = swapped(own)

    inner = inner_products(index_of("zl"), own, columns)
    inner = summed_copies(exchange(inner, ("zl", "c"), 2), 1)[0]
    right, gram = feedback_right(half, own, other, feedback, 4)
    inner, right = lax.optimization_barrier((inner, right))
    right = add_grads(half, inner, swapped(inner), grads_out, right, outer)
    inverse = inverse_factor(gram)
    right = summed_copies(exchange(right, XY), outer)
    right = exchange(right, XY)
    decompressed, right = finish(index_of(XY), half, inverse, own, other, right, width)
    return decompressed, right.T


def solution(mesh):
    outer, tp = mesh.shape["outer"], mesh.shape["tp"]
    across = 4 if outer == 16 else 2
    near = 4 if tp == 32 else 2
    names = ("x", "y", "zh", "zl", "c")
    shape = (outer // across, across, tp // (2 * near), near, 2)
    split_mesh = Mesh(mesh.devices.reshape(shape), names)
    z = ("zh", "zl", "c")
    return jax.shard_map(
        per_device,
        mesh=split_mesh,
        in_specs=(P(XY, z), P(XY, z), P(XY, z), P(z, None)),
        out_specs=(P(XY, z), P(z, None)),
        check_vma=False,
    )
```

```python
import jax
import jax.numpy as jnp
from jax import lax
from jax.experimental import pallas as pl
from jax.experimental.pallas import tpu as pltpu
from jax.sharding import Mesh
from jax.sharding import PartitionSpec as P

F32 = jnp.float32
BF16 = jnp.bfloat16
LANES = 128
FIRST_STEPS = 24
XY = ("x", "y")
FAST = dict(preferred_element_type=F32)
FULL = dict(preferred_element_type=F32, precision=lax.Precision.HIGHEST)


def nn(a, b, kind=FAST):
    return lax.dot_general(a, b, (((1,), (0,)), ((), ())), **kind)


def nt(a, b, kind=FAST):
    return lax.dot_general(a, b, (((1,), (1,)), ((), ())), **kind)


def tn(a, b, kind=FAST):
    return lax.dot_general(a, b, (((0,), (0,)), ((), ())), **kind)


def pieces(value):
    high = value.astype(BF16)
    rest = value - high.astype(F32)
    middle = rest.astype(BF16)
    low = (rest - middle.astype(F32)).astype(BF16)
    return jnp.concatenate([high, middle, low], axis=0)


def folded(stacked):
    third = stacked.shape[0] // 3
    return stacked[:third] + (stacked[third : 2 * third] + stacked[2 * third :])


PARAMS = pltpu.CompilerParams(vmem_limit_bytes=16 * 1024 * 1024)


def cost(flops, count):
    return pl.CostEstimate(flops=flops, bytes_accessed=count, transcendentals=0)


def joined(odd, own, other):
    return jnp.concatenate([jnp.where(odd, other, own), jnp.where(odd, own, other)], axis=0)


def whole_specs(count):
    scalar = pl.BlockSpec(memory_space=pltpu.SMEM)
    return [scalar] + [pl.BlockSpec(memory_space=pltpu.VMEM)] * count


def added_tail(one, two):
    blocks = two.shape[0]

    def kernel(one_ref, two_ref, out_ref):
        tail = jnp.concatenate([two_ref[blocks - 2], two_ref[blocks - 1]], axis=1)
        out_ref[...] = one_ref[...] + tail

    return pl.pallas_call(
        kernel,
        out_shape=jax.ShapeDtypeStruct(one.shape, F32),
        cost_estimate=cost(one.size, 12 * one.size),
        compiler_params=PARAMS,
        name="added_tail",
    )(one, two)


def fetched(feed_ref, held, sems):
    rows = held.shape[0] // sems.shape[0]
    copies = []
    for i in range(sems.shape[0]):
        part = pl.ds(i * rows, rows)
        copies.append(pltpu.make_async_copy(feed_ref.at[part], held.at[part], sems.at[i]))
        copies[-1].start()
    return copies


def left_products(half, start_right, grads, activations, feedback, chunks, copies_wanted):
    rows, width = feedback.shape
    rank, tokens = start_right.shape[0], grads.shape[0]
    pairs = rows // (2 * LANES * chunks)

    def kernel(half_ref, start_ref, grads_ref, act_ref, feed_ref, *refs):
        inner_ref, own_ref, other_ref, copies_ref, held, sems, start, held_grads, few = refs
        first = [
            pltpu.make_async_copy(start_ref, start, few.at[0]),
            pltpu.make_async_copy(grads_ref, held_grads, few.at[1]),
        ] + [
            pltpu.make_async_copy(act_ref, copies_ref.at[i], few.at[2 + i])
            for i in range(copies_wanted)
        ]
        for copy in first:
            copy.start()
        copies = fetched(feed_ref, held, sems)
        odd = half_ref[0] == 1
        first[0].wait()
        split = pieces(start[...])
        first[1].wait()
        inner = folded(nt(split, held_grads[...]))
        inner_ref[...] = inner
        other_ref[chunks * pairs] = inner[:, :LANES]
        other_ref[chunks * pairs + 1] = inner[:, LANES:]
        for k in range(chunks):
            copies[k].wait()
            part = held[k * (rows // chunks) : (k + 1) * (rows // chunks)]
            result = folded(nt(split, part))
            for i in range(pairs):
                even_rows = result[:, 2 * i * LANES : (2 * i + 1) * LANES]
                odd_rows = result[:, (2 * i + 1) * LANES : (2 * i + 2) * LANES]
                own_ref[k * pairs + i] = jnp.where(odd, odd_rows, even_rows)
                other_ref[k * pairs + i] = jnp.where(odd, even_rows, odd_rows)
        for copy in first[2:]:
            copy.wait()

    small = jax.ShapeDtypeStruct((rank, tokens), F32)
    large = jax.ShapeDtypeStruct((rows // (2 * LANES), rank, LANES), F32)
    longer = jax.ShapeDtypeStruct((rows // (2 * LANES) + 2, rank, LANES), F32)
    repeated = jax.ShapeDtypeStruct((copies_wanted,) + activations.shape, BF16)
    return pl.pallas_call(
        kernel,
        in_specs=whole_specs(0) + [pl.BlockSpec(memory_space=pltpu.HBM)] * 4,
        out_shape=(small, large, longer, repeated),
        scratch_shapes=[
            pltpu.VMEM(feedback.shape, BF16),
            pltpu.SemaphoreType.DMA((chunks,)),
            pltpu.VMEM(start_right.shape, F32),
            pltpu.VMEM(grads.shape, BF16),
            pltpu.SemaphoreType.DMA((2 + copies_wanted,)),
        ],
        cost_estimate=cost(6 * rank * width * rows, 2 * feedback.size + 4 * rows * rank),
        compiler_params=PARAMS,
        name="left_products",
    )(half, start_right, grads, activations, feedback)


def add_activations(place, inner, columns, own, other):
    far_size, tokens, _ = columns.shape
    blocks, rank, _ = own.shape

    def kernel(place_ref, columns_ref, own_ref, other_ref, *refs):
        inner_refs, out_ref = refs[:-1], refs[-1]
        for i in range(blocks):
            out_ref[i] = own_ref[i] + other_ref[i]
        total = inner_refs[0][...]
        for ref in inner_refs[1:]:
            total = total + ref[...]
        across = jnp.concatenate([columns_ref[i] for i in range(far_size)], axis=1)
        extra = folded(nn(pieces(total), across))
        for i in range(far_size):
            group = (i + far_size // 2) % far_size
            block = group * (blocks // far_size) + place_ref[0]
            out_ref[block] = out_ref[block] + extra[:, i * LANES : (i + 1) * LANES]

    return pl.pallas_call(
        kernel,
        in_specs=whole_specs(3 + len(inner)),
        out_shape=jax.ShapeDtypeStruct(own.shape, F32),
        cost_estimate=cost(24 * rank * tokens * LANES, 12 * own.size),
        compiler_params=PARAMS,
        name="add_activations",
    )(place, columns, own, other, *inner)


def summed_copies(shares, copies):
    ways, rows, lanes = shares.shape

    def kernel(shares_ref, out_ref):
        total = shares_ref[0]
        for i in range(1, ways):
            total = total + shares_ref[i]
        for i in range(copies):
            out_ref[i] = total

    return pl.pallas_call(
        kernel,
        out_shape=jax.ShapeDtypeStruct((copies, rows, lanes), F32),
        cost_estimate=cost(shares.size, 4 * shares.size),
        compiler_params=PARAMS,
        name="summed_copies",
    )(shares)


def inner_products(near, left, columns):
    blocks, rank, _ = left.shape
    far_size, tokens, _ = columns.shape

    def kernel(near_ref, left_ref, columns_ref, out_ref):
        near_size = blocks // far_size
        groups = [(i + far_size // 2) % far_size for i in range(far_size)]
        rows = [left_ref[group * near_size + near_ref[0]] for group in groups]
        across = jnp.concatenate([columns_ref[i] for i in range(far_size)], axis=1)
        result = folded(nt(pieces(jnp.concatenate(rows, axis=1)), across))
        for i in range(near_size):
            out_ref[2 * i] = result[rank // 2 :]
            out_ref[2 * i + 1] = result[: rank // 2]

    return pl.pallas_call(
        kernel,
        in_specs=whole_specs(2),
        out_shape=jax.ShapeDtypeStruct((2 * blocks // far_size, rank // 2, tokens), F32),
        cost_estimate=cost(6 * rank * tokens * far_size * LANES, 2 * columns.size),
        compiler_params=PARAMS,
        name="inner_products",
    )(near, left, columns)


def feedback_right(half, own, other, feedback, chunks):
    blocks, rank, _ = own.shape
    rows, width = feedback.shape
    pairs = blocks // chunks

    def kernel(half_ref, own_ref, other_ref, feed_ref, out_ref, gram_ref, held, sems):
        copies = fetched(feed_ref, held, sems)
        odd = half_ref[0] == 1
        right = jnp.zeros((rank, width), F32)
        square = jnp.zeros((rank, 3 * rank), F32)
        for k in range(chunks):
            row_blocks = []
            for i in range(k * pairs, (k + 1) * pairs):
                row_blocks.append(jnp.where(odd, other_ref[i], own_ref[i]))
                row_blocks.append(jnp.where(odd, own_ref[i], other_ref[i]))
            split = pieces(jnp.concatenate(row_blocks, axis=1))
            square = square + folded(nt(split, split))
            copies[k].wait()
            part = held[k * (rows // chunks) : (k + 1) * (rows // chunks)]
            right = right + folded(nn(split, part))
        out_ref[...] = right
        gram_ref[...] = square[:, :rank] + square[:, rank : 2 * rank] + square[:, 2 * rank :]

    return pl.pallas_call(
        kernel,
        in_specs=whole_specs(2) + [pl.BlockSpec(memory_space=pltpu.HBM)],
        out_shape=(
            jax.ShapeDtypeStruct((rank, width), F32),
            jax.ShapeDtypeStruct((rank, rank), F32),
        ),
        scratch_shapes=[pltpu.VMEM(feedback.shape, BF16), pltpu.SemaphoreType.DMA((chunks,))],
        cost_estimate=cost(6 * rank * rows * (width + 3 * rank), 2 * feedback.size),
        compiler_params=PARAMS,
        name="feedback_right",
    )(half, own, other, feedback)


def add_grads(half, inner, inner_other, grads, partial, parts):
    rank, width = partial.shape
    tokens = grads.shape[0]
    split_rows = rank * width // (256 * parts)
    across = width // 256

    def kernel(half_ref, inner_ref, inner_other_ref, grads_ref, partial_ref, out_ref):
        inner = joined(half_ref[0] == 1, inner_ref[...], inner_other_ref[...])
        total = partial_ref[...] + folded(nn(pieces(inner), grads_ref[...]))
        for i in range(parts):
            down, over = i // across * split_rows, i % across * 256
            out_ref[i] = total[down : down + split_rows, over : over + 256]

    return pl.pallas_call(
        kernel,
        in_specs=whole_specs(4),
        out_shape=jax.ShapeDtypeStruct((parts, split_rows, 256), F32),
        cost_estimate=cost(6 * rank * tokens * width, 8 * inner.size + 2 * grads.size),
        compiler_params=PARAMS,
        name="add_grads",
    )(half, inner, inner_other, grads, partial)


def eliminated(work, first, last):
    rank = work.shape[0]
    index = lax.broadcasted_iota(jnp.int32, (rank, 1), 0)
    for k in range(first, last):
        low = k // 8 * 8
        pivot_row = work[k : k + 1]
        scale = 1.0 / work[k : k + 1, k : k + 1]
        part = work[low:]
        factor = jnp.where(index[low:] > k, part[:, k : k + 1] * scale, 0.0)
        part = part - factor * pivot_row
        work = part if low == 0 else jnp.concatenate([work[:low], part], axis=0)
    return work


def first_steps(gram):
    rank = gram.shape[0]

    def kernel(gram_ref, out_ref):
        row = lax.broadcasted_iota(jnp.int32, (rank, rank), 0)
        col = lax.broadcasted_iota(jnp.int32, (rank, rank), 1)
        work = jnp.concatenate([gram_ref[...], (row == col).astype(F32)], axis=1)
        out_ref[...] = eliminated(work, 0, FIRST_STEPS)

    return pl.pallas_call(
        kernel,
        out_shape=jax.ShapeDtypeStruct((rank, 2 * rank), F32),
        cost_estimate=cost(8 * rank * rank * rank, 12 * rank * rank),
        compiler_params=PARAMS,
        name="first_steps",
    )(gram)


def inverse_factor(work):
    rank = work.shape[0]

    def kernel(work_ref, out_ref):
        row = lax.broadcasted_iota(jnp.int32, (rank, rank), 0)
        col = lax.broadcasted_iota(jnp.int32, (rank, rank), 1)
        work = eliminated(work_ref[...], FIRST_STEPS, rank)
        diagonal = jnp.sum(jnp.where(row == col, work[:, :rank], 0.0), axis=1, keepdims=True)
        out_ref[...] = work[:, rank:] / jnp.sqrt(diagonal)

    return pl.pallas_call(
        kernel,
        out_shape=jax.ShapeDtypeStruct((rank, rank), F32),
        cost_estimate=cost(8 * rank * rank * rank, 12 * rank * rank),
        compiler_params=PARAMS,
        name="inverse_factor",
    )(work)


def finish(place, half, inverse, own, other, gathered, width):
    rank = inverse.shape[0]
    parts = gathered.shape[0]
    across = width // 256
    slab = 2 * LANES

    def kernel(place_ref, half_ref, inverse_ref, own_ref, other_ref, gathered_ref, dec_ref, right_ref):
        across_rows = [
            jnp.concatenate([gathered_ref[i + j] for j in range(across)], axis=1)
            for i in range(0, parts, across)
        ]
        right = nn(inverse_ref[...], jnp.concatenate(across_rows, axis=0), FULL)
        right_ref[...] = right
        odd = half_ref[0] == 1
        even_rows = jnp.where(odd, other_ref[0], own_ref[0])
        odd_rows = jnp.where(odd, own_ref[0], other_ref[0])
        basis = nn(inverse_ref[...], jnp.concatenate([even_rows, odd_rows], axis=1), FULL)
        dec_ref[...] = tn(basis, right, FULL).astype(BF16)

    block = pl.BlockSpec((1, rank, LANES), lambda i, place, half: (place[0], 0, 0))
    return pl.pallas_call(
        kernel,
        grid_spec=pltpu.PrefetchScalarGridSpec(
            num_scalar_prefetch=2,
            grid=(1,),
            in_specs=[
                pl.BlockSpec(inverse.shape, lambda i, place, half: (0, 0)),
                block,
                block,
                pl.BlockSpec(gathered.shape, lambda i, place, half: (0, 0, 0)),
            ],
            out_specs=[
                pl.BlockSpec((slab, width), lambda i, place, half: (0, 0)),
                pl.BlockSpec((rank, width), lambda i, place, half: (0, 0)),
            ],
        ),
        out_shape=(
            jax.ShapeDtypeStruct((slab, width), BF16),
            jax.ShapeDtypeStruct((rank, width), F32),
        ),
        cost_estimate=cost(12 * rank * slab * width, 4 * gathered.size),
        compiler_params=PARAMS,
        name="finish",
    )(place, half, inverse, own, other, gathered)


def exchange(value, axes, first=0):
    size = lax.axis_size(axes)
    order = [(i + first) % size for i in range(size)]
    return lax.all_to_all(value, axes, 0, 0, axis_index_groups=[order], tiled=True)


def in_hbm(value):
    return pltpu.with_memory_space_constraint(value, pltpu.HBM)


def index_of(axes):
    return lax.axis_index(axes).astype(jnp.int32).reshape(1)


def swapped(value):
    return lax.ppermute(value, "c", [(0, 1), (1, 0)])


def per_device(activations, grads_out, feedback, start_right):
    width = grads_out.shape[1]
    far, near = lax.axis_size("zh"), lax.axis_size("zl")
    outer = lax.axis_size(XY)
    opposite = lax.axis_size("x") // 2 * lax.axis_size("y") + lax.axis_size("y") // 2
    half = index_of("c")
    feedback = in_hbm(feedback)

    inner, own, other, columns = left_products(
        half, in_hbm(start_right.T), in_hbm(grads_out), in_hbm(activations), feedback, 4, far
    )
    columns = exchange(columns, "zh", far // 2)
    other = swapped(other)
    inner = added_tail(inner, other)
    inner = [inner] + [
        lax.ppermute(inner, "zl", [((i + j) % near, i) for i in range(near)])
        for j in range(1, near)
    ]
    left = add_activations(index_of("zl"), inner, columns, own, other)

    left = summed_copies(exchange(left, XY, opposite), near)
    left = summed_copies(exchange(left, "zl", 1), far)
    left = summed_copies(exchange(left, "zh", far // 2), outer)
    own = exchange(left, XY, opposite)
    other = swapped(own)

    inner = inner_products(index_of("zl"), own, columns)
    inner = summed_copies(exchange(inner, ("zl", "c"), 3), 1)[0]
    right, gram = feedback_right(half, own, other, feedback, 4)
    inner, right = lax.optimization_barrier((inner, right))
    right = add_grads(half, inner, swapped(inner), grads_out, right, outer)
    right, work = lax.optimization_barrier((exchange(right, XY, opposite), first_steps(gram)))
    right = summed_copies(right, outer)
    inverse = inverse_factor(work)
    right = exchange(right, XY, opposite)
    decompressed, right = finish(index_of(XY), half, inverse, own, other, right, width)
    return decompressed, right.T


def solution(mesh):
    outer, tp = mesh.shape["outer"], mesh.shape["tp"]
    across = 4 if outer == 16 else 2
    near = 4 if tp == 32 else 2
    names = ("x", "y", "zh", "zl", "c")
    shape = (outer // across, across, tp // (2 * near), near, 2)
    split_mesh = Mesh(mesh.devices.reshape(shape), names)
    z = ("zh", "zl", "c")
    return jax.shard_map(
        per_device,
        mesh=split_mesh,
        in_specs=(P(XY, z), P(XY, z), P(XY, z), P(z, None)),
        out_specs=(P(XY, z), P(z, None)),
        check_vma=False,
    )
```

```python
import jax
import jax.numpy as jnp
from jax import lax
from jax.experimental import pallas as pl
from jax.experimental.pallas import tpu as pltpu
from jax.sharding import Mesh
from jax.sharding import PartitionSpec as P

F32 = jnp.float32
BF16 = jnp.bfloat16
LANES = 128
FIRST_STEPS = 24
XY = ("x", "y")
FAST = dict(preferred_element_type=F32)
FULL = dict(preferred_element_type=F32, precision=lax.Precision.HIGHEST)


def nn(a, b, kind=FAST):
    return lax.dot_general(a, b, (((1,), (0,)), ((), ())), **kind)


def nt(a, b, kind=FAST):
    return lax.dot_general(a, b, (((1,), (1,)), ((), ())), **kind)


def tn(a, b, kind=FAST):
    return lax.dot_general(a, b, (((0,), (0,)), ((), ())), **kind)


def pieces(value):
    high = value.astype(BF16)
    rest = value - high.astype(F32)
    middle = rest.astype(BF16)
    low = (rest - middle.astype(F32)).astype(BF16)
    return jnp.concatenate([high, middle, low], axis=0)


def folded(stacked):
    third = stacked.shape[0] // 3
    return stacked[:third] + (stacked[third : 2 * third] + stacked[2 * third :])


PARAMS = pltpu.CompilerParams(vmem_limit_bytes=16 * 1024 * 1024)


def cost(flops, count):
    return pl.CostEstimate(flops=flops, bytes_accessed=count, transcendentals=0)


def joined(odd, own, other):
    return jnp.concatenate([jnp.where(odd, other, own), jnp.where(odd, own, other)], axis=0)


def whole_specs(count):
    scalar = pl.BlockSpec(memory_space=pltpu.SMEM)
    return [scalar] + [pl.BlockSpec(memory_space=pltpu.VMEM)] * count


def added_tail(one, two):
    blocks = two.shape[0]

    def kernel(one_ref, two_ref, out_ref):
        tail = jnp.concatenate([two_ref[blocks - 2], two_ref[blocks - 1]], axis=1)
        out_ref[...] = one_ref[...] + tail

    return pl.pallas_call(
        kernel,
        out_shape=jax.ShapeDtypeStruct(one.shape, F32),
        cost_estimate=cost(one.size, 12 * one.size),
        compiler_params=PARAMS,
        name="added_tail",
    )(one, two)


def fetched(feed_ref, held, sems):
    rows = held.shape[0] // sems.shape[0]
    copies = []
    for i in range(sems.shape[0]):
        part = pl.ds(i * rows, rows)
        copies.append(pltpu.make_async_copy(feed_ref.at[part], held.at[part], sems.at[i]))
        copies[-1].start()
    return copies


def left_products(half, start_right, grads, activations, feedback, chunks, copies_wanted):
    rows, width = feedback.shape
    rank, tokens = start_right.shape[0], grads.shape[0]
    pairs = rows // (2 * LANES * chunks)

    def kernel(half_ref, start_ref, grads_ref, act_ref, feed_ref, *refs):
        inner_ref, own_ref, other_ref, copies_ref, held, sems, start, held_grads, few = refs
        first = [
            pltpu.make_async_copy(start_ref, start, few.at[0]),
            pltpu.make_async_copy(grads_ref, held_grads, few.at[1]),
        ] + [
            pltpu.make_async_copy(act_ref, copies_ref.at[i], few.at[2 + i])
            for i in range(copies_wanted)
        ]
        for copy in first:
            copy.start()
        copies = fetched(feed_ref, held, sems)
        odd = half_ref[0] == 1
        first[0].wait()
        split = pieces(start[...])
        first[1].wait()
        inner = folded(nt(split, held_grads[...]))
        inner_ref[...] = inner
        other_ref[chunks * pairs] = inner[:, :LANES]
        other_ref[chunks * pairs + 1] = inner[:, LANES:]
        for k in range(chunks):
            copies[k].wait()
            part = held[k * (rows // chunks) : (k + 1) * (rows // chunks)]
            result = folded(nt(split, part))
            for i in range(pairs):
                even_rows = result[:, 2 * i * LANES : (2 * i + 1) * LANES]
                odd_rows = result[:, (2 * i + 1) * LANES : (2 * i + 2) * LANES]
                own_ref[k * pairs + i] = jnp.where(odd, odd_rows, even_rows)
                other_ref[k * pairs + i] = jnp.where(odd, even_rows, odd_rows)
        for copy in first[2:]:
            copy.wait()

    small = jax.ShapeDtypeStruct((rank, tokens), F32)
    large = jax.ShapeDtypeStruct((rows // (2 * LANES), rank, LANES), F32)
    longer = jax.ShapeDtypeStruct((rows // (2 * LANES) + 2, rank, LANES), F32)
    repeated = jax.ShapeDtypeStruct((copies_wanted,) + activations.shape, BF16)
    return pl.pallas_call(
        kernel,
        in_specs=whole_specs(0) + [pl.BlockSpec(memory_space=pltpu.HBM)] * 4,
        out_shape=(small, large, longer, repeated),
        scratch_shapes=[
            pltpu.VMEM(feedback.shape, BF16),
            pltpu.SemaphoreType.DMA((chunks,)),
            pltpu.VMEM(start_right.shape, F32),
            pltpu.VMEM(grads.shape, BF16),
            pltpu.SemaphoreType.DMA((2 + copies_wanted,)),
        ],
        cost_estimate=cost(6 * rank * width * rows, 2 * feedback.size + 4 * rows * rank),
        compiler_params=PARAMS,
        name="left_products",
    )(half, start_right, grads, activations, feedback)


def add_activations(place, inner, columns, own, other):
    far_size, tokens, _ = columns.shape
    blocks, rank, _ = own.shape

    def kernel(place_ref, columns_ref, own_ref, other_ref, *refs):
        inner_refs, out_ref = refs[:-1], refs[-1]
        for i in range(blocks):
            out_ref[i] = own_ref[i] + other_ref[i]
        total = inner_refs[0][...]
        for ref in inner_refs[1:]:
            total = total + ref[...]
        across = jnp.concatenate([columns_ref[i] for i in range(far_size)], axis=1)
        extra = folded(nn(pieces(total), across))
        for i in range(far_size):
            group = (i + far_size // 2) % far_size
            block = group * (blocks // far_size) + place_ref[0]
            out_ref[block] = out_ref[block] + extra[:, i * LANES : (i + 1) * LANES]

    return pl.pallas_call(
        kernel,
        in_specs=whole_specs(3 + len(inner)),
        out_shape=jax.ShapeDtypeStruct(own.shape, F32),
        cost_estimate=cost(24 * rank * tokens * LANES, 12 * own.size),
        compiler_params=PARAMS,
        name="add_activations",
    )(place, columns, own, other, *inner)


def summed_copies(shares, copies):
    ways, rows, lanes = shares.shape

    def kernel(shares_ref, out_ref):
        total = shares_ref[0]
        for i in range(1, ways):
            total = total + shares_ref[i]
        for i in range(copies):
            out_ref[i] = total

    return pl.pallas_call(
        kernel,
        out_shape=jax.ShapeDtypeStruct((copies, rows, lanes), F32),
        cost_estimate=cost(shares.size, 4 * shares.size),
        compiler_params=PARAMS,
        name="summed_copies",
    )(shares)


def inner_products(near, left, columns):
    blocks, rank, _ = left.shape
    far_size, tokens, _ = columns.shape

    def kernel(near_ref, left_ref, columns_ref, out_ref):
        near_size = blocks // far_size
        groups = [(i + far_size // 2) % far_size for i in range(far_size)]
        rows = [left_ref[group * near_size + near_ref[0]] for group in groups]
        across = jnp.concatenate([columns_ref[i] for i in range(far_size)], axis=1)
        result = folded(nt(pieces(jnp.concatenate(rows, axis=1)), across))
        for i in range(near_size):
            out_ref[2 * i] = result[rank // 2 :]
            out_ref[2 * i + 1] = result[: rank // 2]

    return pl.pallas_call(
        kernel,
        in_specs=whole_specs(2),
        out_shape=jax.ShapeDtypeStruct((2 * blocks // far_size, rank // 2, tokens), F32),
        cost_estimate=cost(6 * rank * tokens * far_size * LANES, 2 * columns.size),
        compiler_params=PARAMS,
        name="inner_products",
    )(near, left, columns)


def feedback_right(half, own, other, feedback, chunks):
    blocks, rank, _ = own.shape
    rows, width = feedback.shape
    pairs = blocks // chunks

    def kernel(half_ref, own_ref, other_ref, feed_ref, out_ref, gram_ref, held, sems):
        copies = fetched(feed_ref, held, sems)
        odd = half_ref[0] == 1
        right = jnp.zeros((rank, width), F32)
        square = jnp.zeros((rank, 3 * rank), F32)
        for k in range(chunks):
            row_blocks = []
            for i in range(k * pairs, (k + 1) * pairs):
                row_blocks.append(jnp.where(odd, other_ref[i], own_ref[i]))
                row_blocks.append(jnp.where(odd, own_ref[i], other_ref[i]))
            split = pieces(jnp.concatenate(row_blocks, axis=1))
            square = square + folded(nt(split, split))
            copies[k].wait()
            part = held[k * (rows // chunks) : (k + 1) * (rows // chunks)]
            right = right + folded(nn(split, part))
        out_ref[...] = right
        gram_ref[...] = square[:, :rank] + square[:, rank : 2 * rank] + square[:, 2 * rank :]

    return pl.pallas_call(
        kernel,
        in_specs=whole_specs(2) + [pl.BlockSpec(memory_space=pltpu.HBM)],
        out_shape=(
            jax.ShapeDtypeStruct((rank, width), F32),
            jax.ShapeDtypeStruct((rank, rank), F32),
        ),
        scratch_shapes=[pltpu.VMEM(feedback.shape, BF16), pltpu.SemaphoreType.DMA((chunks,))],
        cost_estimate=cost(6 * rank * rows * (width + 3 * rank), 2 * feedback.size),
        compiler_params=PARAMS,
        name="feedback_right",
    )(half, own, other, feedback)


def add_grads(half, inner, inner_other, grads, partial, parts):
    rank, width = partial.shape
    tokens = grads.shape[0]
    split_rows = rank * width // (256 * parts)
    across = width // 256

    def kernel(half_ref, inner_ref, inner_other_ref, grads_ref, partial_ref, out_ref):
        inner = joined(half_ref[0] == 1, inner_ref[...], inner_other_ref[...])
        total = partial_ref[...] + folded(nn(pieces(inner), grads_ref[...]))
        for i in range(parts):
            down, over = i // across * split_rows, i % across * 256
            out_ref[i] = total[down : down + split_rows, over : over + 256]

    return pl.pallas_call(
        kernel,
        in_specs=whole_specs(4),
        out_shape=jax.ShapeDtypeStruct((parts, split_rows, 256), F32),
        cost_estimate=cost(6 * rank * tokens * width, 8 * inner.size + 2 * grads.size),
        compiler_params=PARAMS,
        name="add_grads",
    )(half, inner, inner_other, grads, partial)


def eliminated(work, first, last):
    rank = work.shape[0]
    index = lax.broadcasted_iota(jnp.int32, (rank, 1), 0)
    for k in range(first, last):
        low = k // 8 * 8
        pivot_row = work[k : k + 1]
        scale = 1.0 / work[k : k + 1, k : k + 1]
        part = work[low:]
        factor = jnp.where(index[low:] > k, part[:, k : k + 1] * scale, 0.0)
        part = part - factor * pivot_row
        work = part if low == 0 else jnp.concatenate([work[:low], part], axis=0)
    return work


def first_steps(gram):
    rank = gram.shape[0]

    def kernel(gram_ref, out_ref):
        row = lax.broadcasted_iota(jnp.int32, (rank, rank), 0)
        col = lax.broadcasted_iota(jnp.int32, (rank, rank), 1)
        work = jnp.concatenate([gram_ref[...], (row == col).astype(F32)], axis=1)
        out_ref[...] = eliminated(work, 0, FIRST_STEPS)

    return pl.pallas_call(
        kernel,
        out_shape=jax.ShapeDtypeStruct((rank, 2 * rank), F32),
        cost_estimate=cost(8 * rank * rank * rank, 12 * rank * rank),
        compiler_params=PARAMS,
        name="first_steps",
    )(gram)


def inverse_factor(work):
    rank = work.shape[0]

    def kernel(work_ref, out_ref):
        row = lax.broadcasted_iota(jnp.int32, (rank, rank), 0)
        col = lax.broadcasted_iota(jnp.int32, (rank, rank), 1)
        work = eliminated(work_ref[...], FIRST_STEPS, rank)
        diagonal = jnp.sum(jnp.where(row == col, work[:, :rank], 0.0), axis=1, keepdims=True)
        out_ref[...] = work[:, rank:] / jnp.sqrt(diagonal)

    return pl.pallas_call(
        kernel,
        out_shape=jax.ShapeDtypeStruct((rank, rank), F32),
        cost_estimate=cost(8 * rank * rank * rank, 12 * rank * rank),
        compiler_params=PARAMS,
        name="inverse_factor",
    )(work)


def finish(place, half, inverse, own, other, gathered, width):
    rank = inverse.shape[0]
    parts = gathered.shape[0]
    across = width // 256
    slab = 2 * LANES

    def kernel(place_ref, half_ref, inverse_ref, own_ref, other_ref, gathered_ref, dec_ref, right_ref):
        across_rows = [
            jnp.concatenate([gathered_ref[i + j] for j in range(across)], axis=1)
            for i in range(0, parts, across)
        ]
        right = nn(inverse_ref[...], jnp.concatenate(across_rows, axis=0), FULL)
        right_ref[...] = right
        odd = half_ref[0] == 1
        even_rows = jnp.where(odd, other_ref[0], own_ref[0])
        odd_rows = jnp.where(odd, own_ref[0], other_ref[0])
        basis = nn(inverse_ref[...], jnp.concatenate([even_rows, odd_rows], axis=1), FULL)
        dec_ref[...] = tn(basis, right, FULL).astype(BF16)

    block = pl.BlockSpec((1, rank, LANES), lambda i, place, half: (place[0], 0, 0))
    return pl.pallas_call(
        kernel,
        grid_spec=pltpu.PrefetchScalarGridSpec(
            num_scalar_prefetch=2,
            grid=(1,),
            in_specs=[
                pl.BlockSpec(inverse.shape, lambda i, place, half: (0, 0)),
                block,
                block,
                pl.BlockSpec(gathered.shape, lambda i, place, half: (0, 0, 0)),
            ],
            out_specs=[
                pl.BlockSpec((slab, width), lambda i, place, half: (0, 0)),
                pl.BlockSpec((rank, width), lambda i, place, half: (0, 0)),
            ],
        ),
        out_shape=(
            jax.ShapeDtypeStruct((slab, width), BF16),
            jax.ShapeDtypeStruct((rank, width), F32),
        ),
        cost_estimate=cost(12 * rank * slab * width, 4 * gathered.size),
        compiler_params=PARAMS,
        name="finish",
    )(place, half, inverse, own, other, gathered)


def exchange(value, axes, first=0):
    size = lax.axis_size(axes)
    order = [(i + first) % size for i in range(size)]
    return lax.all_to_all(value, axes, 0, 0, axis_index_groups=[order], tiled=True)


def in_hbm(value):
    return pltpu.with_memory_space_constraint(value, pltpu.HBM)


def index_of(axes):
    return lax.axis_index(axes).astype(jnp.int32).reshape(1)


def swapped(value):
    return lax.ppermute(value, "c", [(0, 1), (1, 0)])


def per_device(activations, grads_out, feedback, start_right):
    width = grads_out.shape[1]
    far, near = lax.axis_size("zh"), lax.axis_size("zl")
    outer = lax.axis_size(XY)
    opposite = lax.axis_size("x") // 2 * lax.axis_size("y") + lax.axis_size("y") // 2
    half = index_of("c")
    feedback = in_hbm(feedback)

    inner, own, other, columns = left_products(
        half, in_hbm(start_right.T), in_hbm(grads_out), in_hbm(activations), feedback, 4, far
    )
    columns = exchange(columns, "zh", far // 2)
    other = swapped(other)
    inner = added_tail(inner, other)
    inner = [inner] + [
        lax.ppermute(inner, "zl", [((i + j) % near, i) for i in range(near)])
        for j in range(1, near)
    ]
    left = add_activations(index_of("zl"), inner, columns, own, other)

    left = summed_copies(exchange(left, XY, opposite), near)
    left = summed_copies(exchange(left, "zl", near // 2), far)
    left = summed_copies(exchange(left, "zh", far // 2), outer)
    own = exchange(left, XY, opposite)
    other = swapped(own)

    inner = inner_products(index_of("zl"), own, columns)
    inner = summed_copies(exchange(inner, ("zl", "c"), near + 1), 1)[0]
    right, gram = feedback_right(half, own, other, feedback, 4)
    inner, right = lax.optimization_barrier((inner, right))
    right = add_grads(half, inner, swapped(inner), grads_out, right, outer)
    right, work = lax.optimization_barrier((exchange(right, XY, opposite), first_steps(gram)))
    right = summed_copies(right, outer)
    inverse = inverse_factor(work)
    right = exchange(right, XY, opposite)
    decompressed, right = finish(index_of(XY), half, inverse, own, other, right, width)
    return decompressed, right.T


def solution(mesh):
    outer, tp = mesh.shape["outer"], mesh.shape["tp"]
    across = 4 if outer == 16 else 2
    near = 4 if tp == 32 else 2
    names = ("x", "y", "zh", "zl", "c")
    shape = (outer // across, across, tp // (2 * near), near, 2)
    split_mesh = Mesh(mesh.devices.reshape(shape), names)
    z = ("zh", "zl", "c")
    return jax.shard_map(
        per_device,
        mesh=split_mesh,
        in_specs=(P(XY, z), P(XY, z), P(XY, z), P(z, None)),
        out_specs=(P(XY, z), P(z, None)),
        check_vma=False,
    )
```
